32 devices in a mesh: starts: 2 (over y), gx: 8 (over z, x), gy: 2 (over core).
Axes of the slice: x: 2, y: 2, z: 4, core: 2. Of those that a mesh axis runs over, the one named last changes fastest.
Arguments:
- chi_final: float32 [2, 64, 128, 256], P(None, ('starts', 'gx'), 'gy'), parts along dimension 1, may hold values from -30 to 30
- psi_late: float32 [2, 64, 128, 256], P(None, ('starts', 'gx'), 'gy'), parts along dimension 1, may hold values from -0.7 to 0.7
- psi_early: float32 [2, 64, 128, 256], P(None, ('starts', 'gx'), 'gy'), parts along dimension 1, may hold values from -0.7 to 0.7
- trap: float32 [32, 128, 256], P('gx', 'gy'), may hold values from 0 to 1
- controls: float32 [4, 64, 256], P('starts', 'gy'), parts along dimension 0, may hold values from -0.5 to 0.5
Outputs:
- chi_start: float32 [2, 64, 128, 256], P(None, ('starts', 'gx'), 'gy'), parts along dimension 1
- grad_rows: float32 [4, 64, 256], P('starts', 'gy'), parts along dimension 0
- adjoint_power: float32 [2], P('starts'), parts along dimension 0
The draws below stay inside these ranges and needn't reach their ends.
There are 2 independent parts, one for each index of `starts`. The reference program is written for one: setup_inputs(seed, part) draws one part's arguments, and reference() takes and returns one part's arrays. A program takes and returns all parts, laid end to end along the dimension named above; an argument that names none is the same for every part. Nothing has to cross between parts.
All inputs are finite; a program needn't handle non-finite values.
Results may differ from the reference program's by a relative error of at most 0.0005.
Values sent between devices are 32-bit elements; how exact they have to be, the bound alone decides.
A program may use at most 64 MiB of HBM per device.

```python
import math
import jax
import jax.numpy as jnp
from jax import lax

NX = 32
NY = 128
NZ = 256


def draw_chi_final(key, part):
    key_base = jax.random.fold_in(jax.random.fold_in(key, 11), 0)
    base = jnp.clip(jax.random.normal(key_base, (2, NX, NY, NZ), jnp.float32), -5.0, 5.0)
    position = jnp.arange(NX).astype(jnp.float32) / float(max(NX - 1, 1))
    power = (1.0 + 2.0 * position)[:, None, None] * jnp.ones((1, NY, NZ), jnp.float32)
    return base * jnp.sqrt(power)[None]


def steps_of(rng, extent, pieces, least, largest):
    level = 1.0
    for axis_at, shards_of in pieces:
        draws = jax.random.uniform(jax.random.fold_in(jax.random.fold_in(rng, 6), axis_at), (shards_of,), jnp.float32, least / len(pieces), largest / len(pieces))
        level = level * jnp.repeat(jnp.exp(draws), extent[axis_at] // shards_of).reshape((-1,) + (1,) * (len(extent) - 1 - axis_at))
    return level


def setup_inputs(seed: int = 0, part: int = 0) -> dict:
    streams_of = jax.random.split(jax.random.key(seed), 6)
    part_splits = jax.random.split(jax.random.fold_in(streams_of[5], part), 6)
    chi_final = draw_chi_final(jax.random.fold_in(jax.random.fold_in(streams_of[5], part), 71), part)
    psi_late = jnp.clip(jax.random.uniform(part_splits[1], (2, NX, NY, NZ), jnp.float32, -0.7, 0.7) * steps_of(part_splits[1], (2, NX, NY, NZ), ((1, 8), (2, 2)), -0.4, 0.0), -0.7, 0.7)
    psi_early = jnp.clip(jax.random.uniform(part_splits[2], (2, NX, NY, NZ), jnp.float32, -0.7, 0.7) * steps_of(part_splits[2], (2, NX, NY, NZ), ((1, 8), (2, 2)), -0.4, 0.0), -0.7, 0.7)
    trap = jnp.clip(1.0 * jax.random.uniform(streams_of[3], (NX, NY, NZ), jnp.float32) ** steps_of(streams_of[3], (NX, NY, NZ), ((0, 8), (1, 2)), -0.2, 0.2), 0.0, 1.0)
    controls = jnp.clip(jax.random.uniform(part_splits[4], (2, NY // 2, NZ), jnp.float32, -0.5, 0.5) * steps_of(part_splits[4], (2, NY // 2, NZ), ((1, 2),), -0.4, 0.0), -0.5, 0.5)
    return dict(chi_final=chi_final, psi_late=psi_late, psi_early=psi_early, trap=trap, controls=controls)


COUPLING = 1.0
STEP_SIZE = 0.2

def profile_of(x_index, total):
    return 1.0 + 0.5 * jnp.cos(2.0 * math.pi * x_index / total)

def coefficients(psi, trap, control, profile):
    real_part = psi[0]
    imag_part = psi[1]
    fine_control = jnp.repeat(control, 2, axis=0)
    potential = trap + profile[:, None, None] * fine_control[None, :, :]
    weight = potential + 2.0 * COUPLING * (real_part * real_part + imag_part * imag_part)
    mix_a = COUPLING * (real_part * real_part - imag_part * imag_part)
    mix_b = 2.0 * COUPLING * real_part * imag_part
    return (weight, mix_a, mix_b)

def laplace(field):
    padded = jnp.pad(field, ((0, 0), (1, 1), (1, 1), (1, 1)))
    total = padded[:, 2:, 1:-1, 1:-1] + padded[:, :-2, 1:-1, 1:-1]
    total = total + padded[:, 1:-1, 2:, 1:-1] + padded[:, 1:-1, :-2, 1:-1]
    total = total + padded[:, 1:-1, 1:-1, 2:] + padded[:, 1:-1, 1:-1, :-2]
    return total - 6.0 * field

def operator(field, coef):
    weight, mix_a, mix_b = coef
    lapl = laplace(field)
    real_part = field[0]
    imag_part = field[1]
    upper = -0.5 * lapl[0] + (weight + mix_a) * real_part + mix_b * imag_part
    lower = -0.5 * lapl[1] + mix_b * real_part + (weight - mix_a) * imag_part
    return jnp.stack([-lower, upper])

def rk_step(field, coef):
    section_one = operator(field, coef)
    section_two = operator(field + 0.5 * STEP_SIZE * section_one, coef)
    section_three = operator(field + 0.5 * STEP_SIZE * section_two, coef)
    section_four = operator(field + STEP_SIZE * section_three, coef)
    return field + STEP_SIZE / 6.0 * (section_one + 2.0 * section_two + 2.0 * section_three + section_four)

def row_terms(field, psi, profile):
    intersection = field[0] * psi[1] - field[1] * psi[0]
    summed = lax.optimization_barrier(jnp.sum(intersection * profile[:, None, None], axis=0))
    return summed.reshape(summed.shape[0] // 2, 2, summed.shape[1]).sum(axis=1)

def reference(chi_final, psi_late, psi_early, trap, controls):
    profile = profile_of(jnp.arange(NX).astype(jnp.float32), float(NX))
    chi_late = rk_step(chi_final, coefficients(psi_late, trap, controls[1], profile))
    chi_start = rk_step(chi_late, coefficients(psi_early, trap, controls[0], profile))
    rows = jnp.stack([row_terms(chi_start, psi_early, profile), row_terms(chi_late, psi_late, profile)])
    power = jnp.sum(chi_start * chi_start) / float(NX * NY * NZ)
    grad_rows = rows / jnp.sqrt(float(NX) * (power + 1e-06))
    return (chi_start, grad_rows, jnp.reshape(power, (1,)).astype(jnp.float32))
```

```python
import functools
import math

import jax
import jax.numpy as jnp
from jax import lax
from jax.experimental import pallas as pl
from jax.experimental.pallas import tpu as pltpu
from jax.sharding import PartitionSpec as P

STEP_SIZE = 0.2
MESH = pl.DeviceIdType.MESH


def kernel(
    sections, planes, rows, chi, psi_late, psi_early, trap, controls,
    out, grad, power,
    field, psi, pot, coef, edge_in, edge_out, result, fine, ctl, prof, folded,
    late_rows, early_rows, far_power,
    x_send, x_recv, y_send, y_recv, t_send, t_recv, own_sem, o_send, o_recv,
    l_send, l_recv, e_send, e_recv, f_send, f_recv,
):
    deep, half, coarse = 2 * planes, rows // 2, rows // 4
    depth = chi.shape[3]
    pieces = depth // 128
    group = 2 * sections
    start = lax.axis_index("starts")
    g = lax.axis_index("gx")
    c = lax.axis_index("gy")
    x = lax.rem(g, 2)
    upper = lax.rem(x + c, 2)
    partner = g + 1 - 2 * x
    mine_at = pl.multiple_of(upper * half, half)
    other_at = pl.multiple_of((1 - upper) * half, half)
    mine_planes = x * planes
    other_planes = (1 - x) * planes
    has_low = g >= 2
    has_high = g < sections - 2

    def remote(src, dst, send, recv, to_g, to_c):
        return pltpu.make_async_remote_copy(
            src_ref=src, dst_ref=dst, send_sem=send, recv_sem=recv,
            device_id=(start, to_g, to_c), device_id_type=MESH,
        )

    mine = pl.ds(mine_at, half)
    own = [
        pltpu.make_async_copy(
            chi.at[:, :, mine, :], field.at[0, :, pl.ds(1 + mine_planes, planes)], own_sem.at[0]),
        pltpu.make_async_copy(
            psi_late.at[:, :, mine, :], psi.at[0, :, pl.ds(mine_planes, planes)], own_sem.at[1]),
        pltpu.make_async_copy(
            trap.at[:, mine, :], pot.at[pl.ds(mine_planes, planes)], own_sem.at[2]),
        pltpu.make_async_copy(
            psi_early.at[:, :, mine, :], psi.at[1, :, pl.ds(mine_planes, planes)], own_sem.at[3]),
        pltpu.make_async_copy(controls, ctl, own_sem.at[4]),
    ]
    for copy in own:
        copy.start()

    barrier = pltpu.get_barrier_semaphore()
    here = 2 * g + c

    def greet(d, _):
        there = lax.rem(here + d, group)
        pl.semaphore_signal(
            barrier, inc=1, device_id=(start, there // 2, lax.rem(there, 2)), device_id_type=MESH)
        return 0

    lax.fori_loop(1, group, greet, 0)
    pl.semaphore_wait(barrier, group - 1)

    theirs = pl.ds(other_at, half)

    def trade(src, dst, i):
        return remote(src, dst, t_send.at[i], t_recv.at[i], partner, c)

    def trades(at):
        part = pl.ds(at, planes)
        return [
            trade(chi.at[:, :, theirs, :], field.at[0, :, pl.ds(1 + at, planes)], 0),
            trade(psi_late.at[:, :, theirs, :], psi.at[0, :, part], 1),
            trade(trap.at[:, theirs, :], pot.at[part], 2),
        ] + [
            trade(psi_early.at[:, j, theirs, :], psi.at[1, :, at + j], 3 + j)
            for j in range(planes)
        ]

    sent = trades(mine_planes)
    arriving = trades(other_planes)
    for i in range(3):
        sent[i].start()

    stages = field.shape[0]
    blank = jnp.zeros((half, depth), jnp.float32)

    @pl.when(jnp.logical_not(has_low))
    def _():
        for s in range(stages):
            field[s, 0, 0] = blank
            field[s, 1, 0] = blank

    @pl.when(jnp.logical_not(has_high))
    def _():
        for s in range(stages):
            field[s, 0, deep + 1] = blank
            field[s, 1, deep + 1] = blank

    @pl.when(x == 0)
    def _():
        for s in range(stages):
            edge_in[s, upper] = jnp.zeros((2, deep, depth), jnp.float32)

    def low_copy(s):
        return remote(field.at[s, :, 1], field.at[s, :, deep + 1],
                      x_send.at[s, 0], x_recv.at[s, 1], g - 2, c)

    def high_copy(s):
        return remote(field.at[s, :, deep], field.at[s, :, 0],
                      x_send.at[s, 1], x_recv.at[s, 0], g + 2, c)

    def pair_copy(s):
        return remote(edge_out.at[s, 1 - upper], edge_in.at[s, upper],
                      y_send.at[s, 0], y_recv.at[s, 0], partner, c)

    def core_copy(s):
        return remote(edge_out.at[s, upper], edge_in.at[s, 1 - upper],
                      y_send.at[s, 1], y_recv.at[s, 1], g, 1 - c)

    def pair_arrival(s):
        return remote(edge_out.at[s, 1 - upper], edge_in.at[s, 1 - upper],
                      y_send.at[s, 0], y_recv.at[s, 0], partner, c)

    def core_arrival(s):
        return remote(edge_out.at[s, upper], edge_in.at[s, upper],
                      y_send.at[s, 1], y_recv.at[s, 1], g, 1 - c)

    def send_low(s):
        @pl.when(has_low)
        def _():
            low_copy(s).start()

    def send_high(s):
        @pl.when(has_high)
        def _():
            high_copy(s).start()

    def send_edges(s):
        pair_copy(s).start()

        @pl.when(x == 1)
        def _():
            core_copy(s).start()

    def wait_edges(s):
        pair_arrival(s).wait_recv()

        @pl.when(x == 1)
        def _():
            core_arrival(s).wait_recv()

    def wait_low(s):
        @pl.when(has_low)
        def _():
            high_copy(s).wait_recv()

    def wait_high(s):
        @pl.when(has_high)
        def _():
            low_copy(s).wait_recv()

    index = (g // 2) * deep + lax.broadcasted_iota(jnp.int32, (deep, depth), 0)
    prof[...] = 1.0 + 0.5 * jnp.cos(
        (2.0 * math.pi / (sections * planes)) * index.astype(jnp.float32))
    own[4].wait()
    for k in range(2):
        part = ctl[1 - k, pl.ds(pl.multiple_of(upper * coarse, coarse), coarse), :]
        for m in range(pieces):
            piece = part[:, m * 128:(m + 1) * 128]
            fine[k, m, pl.ds(0, coarse, stride=2), :] = piece
            fine[k, m, pl.ds(1, coarse, stride=2), :] = piece

    def coefficients(k, first):
        control = jnp.concatenate([fine[k, m] for m in range(pieces)], axis=1)

        def body(i, _):
            j = first + i
            p = psi[k, 0, j]
            q = psi[k, 1, j]
            base = pot[j] + prof[pl.ds(j, 1), :] * control + 3.0
            p2 = p * p
            q2 = q * q
            both = base + p2 + q2
            coef[k, 0, j] = STEP_SIZE * (both + 2.0 * p2)
            coef[k, 1, j] = (2.0 * STEP_SIZE) * (p * q)
            coef[k, 2, j] = STEP_SIZE * (both + 2.0 * q2)
            return 0

        lax.fori_loop(0, planes, body, 0)

    row = lax.broadcasted_iota(jnp.int32, (half, depth), 0)
    lane = lax.broadcasted_iota(jnp.int32, (half, depth), 1)
    first_row, last_row = row == 0, row == half - 1
    first_lane, last_lane = lane == 0, lane == depth - 1

    def neighbours(s, part, at, v):
        total = field[s, part, at - 1] + field[s, part, at + 1]
        total += jnp.where(
            first_row, edge_in[s, 0, part, pl.ds(at - 1, 1), :], pltpu.roll(v, 1, 0))
        total += jnp.where(
            last_row, edge_in[s, 1, part, pl.ds(at - 1, 1), :], pltpu.roll(v, half - 1, 0))
        total += jnp.where(first_lane, 0.0, pltpu.roll(v, 1, 1))
        total += jnp.where(last_lane, 0.0, pltpu.roll(v, depth - 1, 1))
        return total

    def term(s, at):
        k, n = s // 4, s % 4
        a = field[s, 0, at]
        b = field[s, 1, at]
        diag_a, mixed, diag_b = coef[k, 0, at - 1], coef[k, 1, at - 1], coef[k, 2, at - 1]
        up = diag_a * a + mixed * b - (0.5 * STEP_SIZE) * neighbours(s, 0, at, a)
        low = mixed * a + diag_b * b - (0.5 * STEP_SIZE) * neighbours(s, 1, at, b)
        a, b = low * (-1.0 / (n + 1)), up * (1.0 / (n + 1))
        if n == 3:
            for m in (3, 2, 1, 0):
                a += field[4 * k + m, 0, at]
                b += field[4 * k + m, 1, at]
        return a, b

    def put_edges(s, at, a, b):
        for part, v in ((0, a), (1, b)):
            edge_out[s, 0, part, pl.ds(at - 1, 1), :] = v[0:1]
            edge_out[s, 1, part, pl.ds(at - 1, 1), :] = v[half - 1:half]

    def overlap(k, at, a, b):
        weight = prof[pl.ds(at - 1, 1), :]
        return weight * (a * psi[k, 1, at - 1] - b * psi[k, 0, at - 1])

    def update(s, at, acc):
        a, b = term(s, at)
        field[s + 1, 0, at] = a
        field[s + 1, 1, at] = b
        put_edges(s + 1, at, a, b)
        if s == 3:
            acc = acc + overlap(0, at, a, b)
        return acc

    def fold(acc):
        for m in range(pieces):
            folded[m] = acc[:, m * 128:(m + 1) * 128]
        return jnp.concatenate(
            [folded[m, pl.ds(0, coarse, stride=2), :] + folded[m, pl.ds(1, coarse, stride=2), :]
             for m in range(pieces)], axis=1)

    own[0].wait()
    arriving[0].wait_recv()

    def first_edges(i, _):
        put_edges(0, i + 1, field[0, 0, i + 1], field[0, 1, i + 1])
        return 0

    send_low(0)
    send_high(0)
    lax.fori_loop(0, deep, first_edges, 0)
    send_edges(0)

    own[1].wait()
    own[2].wait()
    coefficients(0, mine_planes)
    arriving[1].wait_recv()
    arriving[2].wait_recv()
    sent[3].start()
    sent[4].start()
    coefficients(0, other_planes)

    late_sends = lambda d: remote(
        late_rows.at[g], late_rows.at[g], l_send.at[d], l_recv.at[g], lax.rem(g + d, sections), c)
    late_arrival = lambda d: remote(
        late_rows.at[g], late_rows.at[lax.rem(g + d, sections)], l_send.at[d],
        l_recv.at[lax.rem(g + d, sections)], lax.rem(g + d, sections), c)

    def loop(count, action):
        def body(d, _):
            action(d)
            return 0

        lax.fori_loop(1, count, body, 0)

    for s in range(stages - 1):
        acc = blank if s == 3 else 0
        wait_edges(s)
        if s == 3:
            acc = lax.fori_loop(2, deep, lambda at, t, s=s: update(s, at, t), acc)
        else:
            lax.fori_loop(2, deep, lambda at, t, s=s: update(s, at, t), 0)
        wait_low(s)
        acc = update(s, 1, acc)
        send_low(s + 1)
        wait_high(s)
        acc = update(s, deep, acc)
        send_high(s + 1)
        send_edges(s + 1)
        if s < planes - 2:
            sent[5 + s].start()
        if s == 3:
            late_rows[g] = fold(acc)
            loop(sections, lambda d: late_sends(d).start())
            own[3].wait()
            coefficients(1, mine_planes)
            for j in range(planes):
                arriving[3 + j].wait_recv()
            coefficients(1, other_planes)

    s = stages - 1

    def give(j):
        return remote(result.at[:, other_planes + j], out.at[:, j, mine, :],
                      o_send.at[j], o_recv.at[j], partner, c)

    def give_arrival(j):
        return remote(result.at[:, other_planes + j], out.at[:, j, theirs, :],
                      o_send.at[j], o_recv.at[j], partner, c)

    def finish(at, accs):
        acc, square = accs
        a, b = term(s, at)
        result[0, at - 1] = a
        result[1, at - 1] = b
        return acc + overlap(1, at, a, b), square + (a * a + b * b)

    accs = (blank, blank)
    wait_edges(s)
    inner_other = other_planes + x
    inner_mine = mine_planes + 1 - x

    def finish_send(i, accs):
        accs = finish(inner_other + i + 1, accs)
        give(x + i).start()
        return accs

    accs = lax.fori_loop(0, planes - 1, finish_send, accs)
    accs = lax.fori_loop(0, planes - 1, lambda i, t: finish(inner_mine + i + 1, t), accs)
    wait_low(s)
    wait_high(s)
    end_other = (1 - x) * (deep - 1)
    accs = finish(end_other + 1, accs)
    give((1 - x) * (planes - 1)).start()
    accs = finish(x * (deep - 1) + 1, accs)
    keep = pltpu.make_async_copy(
        result.at[:, pl.ds(mine_planes, planes)], out.at[:, :, mine, :], own_sem.at[0])
    keep.start()
    acc, square = accs
    early_rows[g, 0:coarse] = fold(acc)
    early_rows[g, coarse:coarse + 8] = jnp.sum(square.reshape(half // 8, 8, depth), axis=0)

    def early_copy(d, slot):
        return remote(early_rows.at[g], early_rows.at[slot], e_send.at[d], e_recv.at[slot],
                      lax.rem(g + d, sections), c)

    def far_copy(d, slot):
        return remote(early_rows.at[g, pl.ds(coarse, 8)], far_power.at[slot], f_send.at[d],
                      f_recv.at[slot], lax.rem(g + d, sections), 1 - c)

    far_copy(0, g).start()
    loop(sections, lambda d: (early_copy(d, g).start(), far_copy(d, g).start()))

    loop(sections, lambda d: late_arrival(d).wait_recv())

    def total(source, parity):
        value = source[parity, 0:coarse]
        return lax.fori_loop(
            1, sections // 2, lambda i, t: t + source[2 * i + parity, 0:coarse], value)

    late = [total(late_rows, c), total(late_rows, 1 - c)]
    far_copy(0, g).wait_recv()
    loop(sections, lambda d: (
        early_copy(d, lax.rem(g + d, sections)).wait_recv(),
        far_copy(d, lax.rem(g + d, sections)).wait_recv()))

    def squares(i, t):
        near, far = t
        return near + early_rows[i, coarse:coarse + 8], far + far_power[i]

    zero = jnp.zeros((8, depth), jnp.float32)
    near, far = lax.fori_loop(0, sections, squares, (zero, zero))
    mean = jnp.sum(near + far) / float(sections * planes * 2 * rows * depth)
    power[0] = mean
    scale = jnp.sqrt(float(sections * planes) * (jnp.full((coarse, depth), mean) + 1e-06))
    early = [total(early_rows, c), total(early_rows, 1 - c)]
    for i in range(2):
        grad[0, i * coarse:(i + 1) * coarse] = early[i] / scale
        grad[1, i * coarse:(i + 1) * coarse] = late[i] / scale

    for copy in sent:
        copy.wait_send()
    for s in range(stages):
        pair_copy(s).wait_send()

        @pl.when(x == 1)
        def _():
            core_copy(s).wait_send()

        @pl.when(has_low)
        def _():
            low_copy(s).wait_send()

        @pl.when(has_high)
        def _():
            high_copy(s).wait_send()

    loop(sections, lambda d: (late_sends(d).wait_send(), early_copy(d, g).wait_send(),
                              far_copy(d, g).wait_send()))
    far_copy(0, g).wait_send()
    keep.wait()
    for j in range(planes):
        give(j).wait_send()
        give_arrival(j).wait_recv()


def on_device(chi_final, psi_late, psi_early, trap, controls):
    planes, rows, depth = chi_final.shape[1:]
    sections = lax.axis_size("gx")
    deep, half, coarse = 2 * planes, rows // 2, rows // 4
    stages = 8
    f32 = jnp.float32
    anywhere = pl.BlockSpec(memory_space=pl.ANY)
    dma = pltpu.SemaphoreType.DMA
    return pl.pallas_call(
        functools.partial(kernel, sections, planes, rows),
        out_shape=(
            jax.ShapeDtypeStruct(chi_final.shape, f32),
            jax.ShapeDtypeStruct(controls.shape, f32),
            jax.ShapeDtypeStruct((1,), f32),
        ),
        in_specs=[anywhere] * 5,
        out_specs=(
            anywhere,
            pl.BlockSpec(memory_space=pltpu.VMEM),
            pl.BlockSpec(memory_space=pltpu.SMEM),
        ),
        scratch_shapes=[
            pltpu.VMEM((stages, 2, deep + 2, half, depth), f32),
            pltpu.VMEM((2, 2, deep, half, depth), f32),
            pltpu.VMEM((deep, half, depth), f32),
            pltpu.VMEM((2, 3, deep, half, depth), f32),
            pltpu.VMEM((stages, 2, 2, deep, depth), f32),
            pltpu.VMEM((stages, 2, 2, deep, depth), f32),
            pltpu.VMEM((2, deep, half, depth), f32),
            pltpu.VMEM((2, depth // 128, half, 128), f32),
            pltpu.VMEM(controls.shape, f32),
            pltpu.VMEM((deep, depth), f32),
            pltpu.VMEM((depth // 128, half, 128), f32),
            pltpu.VMEM((sections, coarse, depth), f32),
            pltpu.VMEM((sections, coarse + 8, depth), f32),
            pltpu.VMEM((sections, 8, depth), f32),
            dma((stages, 2)), dma((stages, 2)), dma((stages, 2)), dma((stages, 2)),
            dma((3 + planes,)), dma((3 + planes,)), dma((5,)), dma((planes,)), dma((planes,)),
            dma((sections,)), dma((sections,)), dma((sections,)), dma((sections,)),
            dma((sections,)), dma((sections,)),
        ],
        compiler_params=pltpu.CompilerParams(
            collective_id=0, has_side_effects=True, vmem_limit_bytes=32 * 1024 * 1024
        ),
        cost_estimate=pl.CostEstimate(
            flops=400 * planes * rows * depth, bytes_accessed=3_000_000, transcendentals=0),
    )(chi_final, psi_late, psi_early, trap, controls)


def solution(mesh):
    placed = (
        P(None, ("starts", "gx"), "gy", None),
        P(None, ("starts", "gx"), "gy", None),
        P(None, ("starts", "gx"), "gy", None),
        P("gx", "gy", None),
        P("starts", "gy", None),
    )
    return jax.shard_map(
        on_device,
        mesh=mesh,
        in_specs=placed,
        out_specs=(P(None, ("starts", "gx"), "gy", None), P("starts", "gy", None), P("starts")),
        check_vma=False,
    )
```

```python
import functools
import math

import jax
import jax.numpy as jnp
from jax import lax
from jax.experimental import pallas as pl
from jax.experimental.pallas import tpu as pltpu
from jax.sharding import PartitionSpec as P

STEP_SIZE = 0.2
MESH = pl.DeviceIdType.MESH


def kernel(
    sections, planes, rows, chi, psi_late, psi_early, trap, controls,
    out, grad, power,
    field, psi, pot, coef, edge_in, edge_out, rim_in, rim_out, result, fine, ctl, prof, folded,
    late_rows, early_rows, far_power,
    x_send, x_recv, y_send, y_recv, t_send, t_recv, own_sem, o_send, o_recv,
    l_send, l_recv, e_send, e_recv, f_send, f_recv,
):
    deep, half, coarse = 2 * planes, rows // 2, rows // 4
    depth = chi.shape[3]
    pieces = depth // 128
    group = 2 * sections
    start = lax.axis_index("starts")
    g = lax.axis_index("gx")
    c = lax.axis_index("gy")
    x = lax.rem(g, 2)
    upper = lax.rem(x + c, 2)
    partner = g + 1 - 2 * x
    mine_at = pl.multiple_of(upper * half, half)
    other_at = pl.multiple_of((1 - upper) * half, half)
    mine_planes = x * planes
    other_planes = (1 - x) * planes
    has_low = g >= 2
    has_high = g < sections - 2

    def remote(src, dst, send, recv, to_g, to_c):
        return pltpu.make_async_remote_copy(
            src_ref=src, dst_ref=dst, send_sem=send, recv_sem=recv,
            device_id=(start, to_g, to_c), device_id_type=MESH,
        )

    mine = pl.ds(mine_at, half)
    own = [
        pltpu.make_async_copy(
            chi.at[:, :, mine, :], field.at[0, :, pl.ds(1 + mine_planes, planes)], own_sem.at[0]),
        pltpu.make_async_copy(
            psi_late.at[:, :, mine, :], psi.at[0, :, pl.ds(mine_planes, planes)], own_sem.at[1]),
        pltpu.make_async_copy(
            trap.at[:, mine, :], pot.at[pl.ds(mine_planes, planes)], own_sem.at[2]),
        pltpu.make_async_copy(
            psi_early.at[:, :, mine, :], psi.at[1, :, pl.ds(mine_planes, planes)], own_sem.at[3]),
        pltpu.make_async_copy(controls, ctl, own_sem.at[4]),
    ]
    for copy in own:
        copy.start()

    barrier = pltpu.get_barrier_semaphore()
    here = 2 * g + c

    def greet(d, _):
        there = lax.rem(here + d, group)
        pl.semaphore_signal(
            barrier, inc=1, device_id=(start, there // 2, lax.rem(there, 2)), device_id_type=MESH)
        return 0

    lax.fori_loop(1, group, greet, 0)
    pl.semaphore_wait(barrier, group - 1)

    theirs = pl.ds(other_at, half)

    def trade(src, dst, i):
        return remote(src, dst, t_send.at[i], t_recv.at[i], partner, c)

    def trades(at, flag):
        rim = flag * (planes - 1)
        rest = pl.ds(1 - flag, planes - 1)
        rest_to = pl.ds(at + 2 - flag, planes - 1)
        moves = [
            trade(chi.at[:, rim, theirs, :], field.at[0, :, 1 + at + rim], 0),
            trade(chi.at[:, rest, theirs, :], field.at[0, :, rest_to], 1),
        ]
        for j in range(planes):
            moves.append(trade(psi_late.at[:, j, theirs, :], psi.at[0, :, at + j], 2 + 3 * j))
            moves.append(trade(trap.at[j, theirs, :], pot.at[at + j], 3 + 3 * j))
            moves.append(trade(psi_early.at[:, j, theirs, :], psi.at[1, :, at + j], 4 + 3 * j))
        return moves

    sent = trades(mine_planes, x)
    arriving = trades(other_planes, 1 - x)
    sent[0].start()
    sent[1].start()
    for j in range(planes):
        sent[2 + 3 * j].start()
        sent[3 + 3 * j].start()

    stages = field.shape[0]
    blank = jnp.zeros((half, depth), jnp.float32)

    @pl.when(jnp.logical_not(has_low))
    def _():
        for s in range(stages):
            field[s, 0, 0] = blank
            field[s, 1, 0] = blank

    @pl.when(jnp.logical_not(has_high))
    def _():
        for s in range(stages):
            field[s, 0, deep + 1] = blank
            field[s, 1, deep + 1] = blank

    @pl.when(x == 0)
    def _():
        for s in range(stages):
            edge_in[s, upper] = jnp.zeros((2, deep, depth), jnp.float32)
            rim_in[s, upper] = jnp.zeros((8, depth), jnp.float32)

    def low_copy(s, part):
        return remote(field.at[s, part, 1], field.at[s, part, deep + 1],
                      x_send.at[s, 0, part], x_recv.at[s, 1, part], g - 2, c)

    def high_copy(s, part):
        return remote(field.at[s, part, deep], field.at[s, part, 0],
                      x_send.at[s, 1, part], x_recv.at[s, 0, part], g + 2, c)

    boxes = ((edge_out, edge_in), (rim_out, rim_in))

    def pair_copy(s, box):
        source, target = boxes[box]
        return remote(source.at[s, 1 - upper], target.at[s, upper],
                      y_send.at[s, box, 0], y_recv.at[s, box, 0], partner, c)

    def core_copy(s, box):
        source, target = boxes[box]
        return remote(source.at[s, upper], target.at[s, 1 - upper],
                      y_send.at[s, box, 1], y_recv.at[s, box, 1], g, 1 - c)

    def pair_arrival(s, box):
        source, target = boxes[box]
        return remote(source.at[s, 1 - upper], target.at[s, 1 - upper],
                      y_send.at[s, box, 0], y_recv.at[s, box, 0], partner, c)

    def core_arrival(s, box):
        source, target = boxes[box]
        return remote(source.at[s, upper], target.at[s, upper],
                      y_send.at[s, box, 1], y_recv.at[s, box, 1], g, 1 - c)

    def send_low(s):
        @pl.when(has_low)
        def _():
            low_copy(s, 0).start()
            low_copy(s, 1).start()

    def send_high(s):
        @pl.when(has_high)
        def _():
            high_copy(s, 0).start()
            high_copy(s, 1).start()

    def send_edges(s, box):
        pair_copy(s, box).start()

        @pl.when(x == 1)
        def _():
            core_copy(s, box).start()

    def wait_edges(s, box):
        pair_arrival(s, box).wait_recv()

        @pl.when(x == 1)
        def _():
            core_arrival(s, box).wait_recv()

    def wait_low(s):
        @pl.when(has_low)
        def _():
            high_copy(s, 0).wait_recv()
            high_copy(s, 1).wait_recv()

    def wait_high(s):
        @pl.when(has_high)
        def _():
            low_copy(s, 0).wait_recv()
            low_copy(s, 1).wait_recv()

    index = (g // 2) * deep + lax.broadcasted_iota(jnp.int32, (deep, depth), 0)
    prof[...] = 1.0 + 0.5 * jnp.cos(
        (2.0 * math.pi / (sections * planes)) * index.astype(jnp.float32))
    own[4].wait()
    for k in range(2):
        part = ctl[1 - k, pl.ds(pl.multiple_of(upper * coarse, coarse), coarse), :]
        for m in range(pieces):
            piece = part[:, m * 128:(m + 1) * 128]
            fine[k, m, pl.ds(0, coarse, stride=2), :] = piece
            fine[k, m, pl.ds(1, coarse, stride=2), :] = piece

    def coefficients(k, first, count):
        control = jnp.concatenate([fine[k, m] for m in range(pieces)], axis=1)

        def body(i, _):
            j = first + i
            p = psi[k, 0, j]
            q = psi[k, 1, j]
            base = pot[j] + prof[pl.ds(j, 1), :] * control + 3.0
            p2 = p * p
            q2 = q * q
            both = base + p2 + q2
            coef[k, 0, j] = STEP_SIZE * (both + 2.0 * p2)
            coef[k, 1, j] = (2.0 * STEP_SIZE) * (p * q)
            coef[k, 2, j] = STEP_SIZE * (both + 2.0 * q2)
            return 0

        lax.fori_loop(0, count, body, 0)

    row = lax.broadcasted_iota(jnp.int32, (half, depth), 0)
    lane = lax.broadcasted_iota(jnp.int32, (half, depth), 1)
    first_row, last_row = row == 0, row == half - 1
    first_lane, last_lane = lane == 0, lane == depth - 1

    def edge_row(s, side, part, at, end):
        if end is None:
            return edge_in[s, side, part, pl.ds(at - 1, 1), :]
        return rim_in[s, side, pl.ds(2 * part + end, 1), :]

    def neighbours(s, part, at, v, end):
        total = field[s, part, at - 1] + field[s, part, at + 1]
        total += jnp.where(
            first_row, edge_row(s, 0, part, at, end), pltpu.roll(v, 1, 0))
        total += jnp.where(
            last_row, edge_row(s, 1, part, at, end), pltpu.roll(v, half - 1, 0))
        total += jnp.where(first_lane, 0.0, pltpu.roll(v, 1, 1))
        total += jnp.where(last_lane, 0.0, pltpu.roll(v, depth - 1, 1))
        return total

    def term(s, at, end):
        k, n = s // 4, s % 4
        a = field[s, 0, at]
        b = field[s, 1, at]
        diag_a, mixed, diag_b = coef[k, 0, at - 1], coef[k, 1, at - 1], coef[k, 2, at - 1]
        up = diag_a * a + mixed * b - (0.5 * STEP_SIZE) * neighbours(s, 0, at, a, end)
        low = mixed * a + diag_b * b - (0.5 * STEP_SIZE) * neighbours(s, 1, at, b, end)
        a, b = low * (-1.0 / (n + 1)), up * (1.0 / (n + 1))
        if n == 3:
            for m in (3, 2, 1, 0):
                a += field[4 * k + m, 0, at]
                b += field[4 * k + m, 1, at]
        return a, b

    def put_edges(s, at, a, b, end):
        for part, v in ((0, a), (1, b)):
            if end is None:
                edge_out[s, 0, part, pl.ds(at - 1, 1), :] = v[0:1]
                edge_out[s, 1, part, pl.ds(at - 1, 1), :] = v[half - 1:half]
            else:
                rim_out[s, 0, pl.ds(2 * part + end, 1), :] = v[0:1]
                rim_out[s, 1, pl.ds(2 * part + end, 1), :] = v[half - 1:half]

    def overlap(k, at, a, b):
        weight = prof[pl.ds(at - 1, 1), :]
        return weight * (a * psi[k, 1, at - 1] - b * psi[k, 0, at - 1])

    def update(s, at, acc, end=None):
        a, b = term(s, at, end)
        field[s + 1, 0, at] = a
        field[s + 1, 1, at] = b
        put_edges(s + 1, at, a, b, end)
        if s == 3:
            acc = acc + overlap(0, at, a, b)
        return acc

    def fold(acc):
        for m in range(pieces):
            folded[m] = acc[:, m * 128:(m + 1) * 128]
        return jnp.concatenate(
            [folded[m, pl.ds(0, coarse, stride=2), :] + folded[m, pl.ds(1, coarse, stride=2), :]
             for m in range(pieces)], axis=1)

    own[0].wait()
    own[1].wait()
    own[2].wait()
    coefficients(0, mine_planes, planes)
    arriving[0].wait_recv()
    send_low(0)
    send_high(0)
    put_edges(0, 1, field[0, 0, 1], field[0, 1, 1], 0)
    put_edges(0, deep, field[0, 0, deep], field[0, 1, deep], 1)
    send_edges(0, 1)
    arriving[1].wait_recv()

    def first_edges(at, _):
        put_edges(0, at, field[0, 0, at], field[0, 1, at], None)
        return 0

    lax.fori_loop(2, deep, first_edges, 0)
    send_edges(0, 0)
    for j in range(planes):
        arriving[2 + 3 * j].wait_recv()
        arriving[3 + 3 * j].wait_recv()
        coefficients(0, other_planes + j, 1)
    sent[4].start()
    sent[7].start()

    late_sends = lambda d: remote(
        late_rows.at[g], late_rows.at[g], l_send.at[d], l_recv.at[g], lax.rem(g + d, sections), c)
    late_arrival = lambda d: remote(
        late_rows.at[g], late_rows.at[lax.rem(g + d, sections)], l_send.at[d],
        l_recv.at[lax.rem(g + d, sections)], lax.rem(g + d, sections), c)

    def loop(count, action):
        def body(d, _):
            action(d)
            return 0

        lax.fori_loop(1, count, body, 0)

    for s in range(stages - 1):
        acc = blank if s == 3 else 0
        wait_edges(s, 0)

        def two(i, acc, s=s):
            acc = update(s, 2 + 2 * i, acc)
            return update(s, 3 + 2 * i, acc)

        acc = lax.fori_loop(0, planes - 1, two, acc)
        send_edges(s + 1, 0)
        wait_edges(s, 1)
        wait_low(s)
        acc = update(s, 1, acc, 0)
        send_low(s + 1)
        wait_high(s)
        acc = update(s, deep, acc, 1)
        send_high(s + 1)
        send_edges(s + 1, 1)
        if s < planes - 2:
            sent[4 + 3 * (2 + s)].start()
        if s == 3:
            late_rows[g] = fold(acc)
            loop(sections, lambda d: late_sends(d).start())
            own[3].wait()
            coefficients(1, mine_planes, planes)
            for j in range(planes):
                arriving[4 + 3 * j].wait_recv()
            coefficients(1, other_planes, planes)

    s = stages - 1

    def give(j):
        return remote(result.at[:, other_planes + j], out.at[:, j, mine, :],
                      o_send.at[j], o_recv.at[j], partner, c)

    def give_arrival(j):
        return remote(result.at[:, other_planes + j], out.at[:, j, theirs, :],
                      o_send.at[j], o_recv.at[j], partner, c)

    def finish(at, accs, end=None):
        acc, square = accs
        a, b = term(s, at, end)
        result[0, at - 1] = a
        result[1, at - 1] = b
        return acc + overlap(1, at, a, b), square + (a * a + b * b)

    accs = (blank, blank)
    wait_edges(s, 0)
    inner_other = other_planes + x
    inner_mine = mine_planes + 1 - x

    def finish_send(i, accs):
        accs = finish(inner_other + i + 1, accs)
        give(x + i).start()
        return accs

    accs = lax.fori_loop(0, planes - 1, finish_send, accs)
    accs = lax.fori_loop(0, planes - 1, lambda i, t: finish(inner_mine + i + 1, t), accs)
    wait_edges(s, 1)
    wait_low(s)
    wait_high(s)
    accs = finish((1 - x) * (deep - 1) + 1, accs, 1 - x)
    give((1 - x) * (planes - 1)).start()
    accs = finish(x * (deep - 1) + 1, accs, x)
    keep = pltpu.make_async_copy(
        result.at[:, pl.ds(mine_planes, planes)], out.at[:, :, mine, :], own_sem.at[0])
    keep.start()
    acc, square = accs
    early_rows[g, 0:coarse] = fold(acc)
    early_rows[g, coarse:coarse + 8] = jnp.sum(square.reshape(half // 8, 8, depth), axis=0)

    def early_copy(d, slot):
        return remote(early_rows.at[g], early_rows.at[slot], e_send.at[d], e_recv.at[slot],
                      lax.rem(g + d, sections), c)

    def far_copy(d, slot):
        return remote(early_rows.at[g, pl.ds(coarse, 8)], far_power.at[slot], f_send.at[d],
                      f_recv.at[slot], lax.rem(g + d, sections), 1 - c)

    far_copy(0, g).start()
    loop(sections, lambda d: (early_copy(d, g).start(), far_copy(d, g).start()))

    loop(sections, lambda d: late_arrival(d).wait_recv())

    def total(source, parity):
        value = source[parity, 0:coarse]
        return lax.fori_loop(
            1, sections // 2, lambda i, t: t + source[2 * i + parity, 0:coarse], value)

    late = [total(late_rows, c), total(late_rows, 1 - c)]
    far_copy(0, g).wait_recv()
    loop(sections, lambda d: (
        early_copy(d, lax.rem(g + d, sections)).wait_recv(),
        far_copy(d, lax.rem(g + d, sections)).wait_recv()))

    def squares(i, t):
        near, far = t
        return near + early_rows[i, coarse:coarse + 8], far + far_power[i]

    zero = jnp.zeros((8, depth), jnp.float32)
    near, far = lax.fori_loop(0, sections, squares, (zero, zero))
    mean = jnp.sum(near + far) / float(sections * planes * 2 * rows * depth)
    power[0] = mean
    scale = jnp.sqrt(float(sections * planes) * (jnp.full((coarse, depth), mean) + 1e-06))
    early = [total(early_rows, c), total(early_rows, 1 - c)]
    for i in range(2):
        grad[0, i * coarse:(i + 1) * coarse] = early[i] / scale
        grad[1, i * coarse:(i + 1) * coarse] = late[i] / scale

    for copy in sent:
        copy.wait_send()
    for s in range(stages):
        for box in range(2):
            pair_copy(s, box).wait_send()

        @pl.when(x == 1)
        def _():
            for box in range(2):
                core_copy(s, box).wait_send()

        @pl.when(has_low)
        def _():
            for part in range(2):
                low_copy(s, part).wait_send()

        @pl.when(has_high)
        def _():
            for part in range(2):
                high_copy(s, part).wait_send()

    loop(sections, lambda d: (late_sends(d).wait_send(), early_copy(d, g).wait_send(),
                              far_copy(d, g).wait_send()))
    far_copy(0, g).wait_send()
    keep.wait()
    for j in range(planes):
        give(j).wait_send()
        give_arrival(j).wait_recv()


def on_device(chi_final, psi_late, psi_early, trap, controls):
    planes, rows, depth = chi_final.shape[1:]
    sections = lax.axis_size("gx")
    deep, half, coarse = 2 * planes, rows // 2, rows // 4
    stages = 8
    f32 = jnp.float32
    anywhere = pl.BlockSpec(memory_space=pltpu.HBM)
    dma = pltpu.SemaphoreType.DMA
    return pl.pallas_call(
        functools.partial(kernel, sections, planes, rows),
        out_shape=(
            jax.ShapeDtypeStruct(chi_final.shape, f32),
            jax.ShapeDtypeStruct(controls.shape, f32),
            jax.ShapeDtypeStruct((1,), f32),
        ),
        in_specs=[anywhere] * 5,
        out_specs=(
            anywhere,
            pl.BlockSpec(memory_space=pltpu.VMEM),
            pl.BlockSpec(memory_space=pltpu.SMEM),
        ),
        scratch_shapes=[
            pltpu.VMEM((stages, 2, deep + 2, half, depth), f32),
            pltpu.VMEM((2, 2, deep, half, depth), f32),
            pltpu.VMEM((deep, half, depth), f32),
            pltpu.VMEM((2, 3, deep, half, depth), f32),
            pltpu.VMEM((stages, 2, 2, deep, depth), f32),
            pltpu.VMEM((stages, 2, 2, deep, depth), f32),
            pltpu.VMEM((stages, 2, 8, depth), f32),
            pltpu.VMEM((stages, 2, 8, depth), f32),
            pltpu.VMEM((2, deep, half, depth), f32),
            pltpu.VMEM((2, depth // 128, half, 128), f32),
            pltpu.VMEM(controls.shape, f32),
            pltpu.VMEM((deep, depth), f32),
            pltpu.VMEM((depth // 128, half, 128), f32),
            pltpu.VMEM((sections, coarse, depth), f32),
            pltpu.VMEM((sections, coarse + 8, depth), f32),
            pltpu.VMEM((sections, 8, depth), f32),
            dma((stages, 2, 2)), dma((stages, 2, 2)), dma((stages, 2, 2)), dma((stages, 2, 2)),
            dma((2 + 3 * planes,)), dma((2 + 3 * planes,)), dma((5,)), dma((planes,)), dma((planes,)),
            dma((sections,)), dma((sections,)), dma((sections,)), dma((sections,)),
            dma((sections,)), dma((sections,)),
        ],
        compiler_params=pltpu.CompilerParams(
            collective_id=0, has_side_effects=True, vmem_limit_bytes=32 * 1024 * 1024
        ),
        cost_estimate=pl.CostEstimate(
            flops=400 * planes * rows * depth, bytes_accessed=3_000_000, transcendentals=0),
    )(chi_final, psi_late, psi_early, trap, controls)


def solution(mesh):
    placed = (
        P(None, ("starts", "gx"), "gy", None),
        P(None, ("starts", "gx"), "gy", None),
        P(None, ("starts", "gx"), "gy", None),
        P("gx", "gy", None),
        P("starts", "gy", None),
    )
    return jax.shard_map(
        on_device,
        mesh=mesh,
        in_specs=placed,
        out_specs=(P(None, ("starts", "gx"), "gy", None), P("starts", "gy", None), P("starts")),
        check_vma=False,
    )
```

```python
import functools
import math

import jax
import jax.numpy as jnp
from jax import lax
from jax.experimental import pallas as pl
from jax.experimental.pallas import tpu as pltpu
from jax.sharding import PartitionSpec as P

STEP_SIZE = 0.2
MESH = pl.DeviceIdType.MESH


def kernel(
    sections, planes, rows, chi, psi_late, psi_early, trap, controls,
    out, grad, power,
    field, psi, pot, coef, edge_in, edge_out, rim_in, rim_out, result, fine, ctl, prof, folded,
    late_rows, early_rows, far_power,
    x_send, x_recv, y_send, y_recv, t_send, t_recv, own_sem, o_send, o_recv,
    l_send, l_recv, e_send, e_recv, f_send, f_recv,
):
    deep, half, coarse = 2 * planes, rows // 2, rows // 4
    depth = chi.shape[3]
    pieces = depth // 128
    group = 2 * sections
    start = lax.axis_index("starts")
    g = lax.axis_index("gx")
    c = lax.axis_index("gy")
    x = lax.rem(g, 2)
    upper = lax.rem(x + c, 2)
    partner = g + 1 - 2 * x
    mine_at = pl.multiple_of(upper * half, half)
    other_at = pl.multiple_of((1 - upper) * half, half)
    mine_planes = x * planes
    other_planes = (1 - x) * planes
    has_low = g >= 2
    has_high = g < sections - 2

    def remote(src, dst, send, recv, to_g, to_c):
        return pltpu.make_async_remote_copy(
            src_ref=src, dst_ref=dst, send_sem=send, recv_sem=recv,
            device_id=(start, to_g, to_c), device_id_type=MESH,
        )

    mine = pl.ds(mine_at, half)
    own = [
        pltpu.make_async_copy(
            chi.at[:, :, mine, :], field.at[0, :, pl.ds(1 + mine_planes, planes)], own_sem.at[0]),
        pltpu.make_async_copy(
            psi_late.at[:, :, mine, :], psi.at[0, :, pl.ds(mine_planes, planes)], own_sem.at[1]),
        pltpu.make_async_copy(
            trap.at[:, mine, :], pot.at[pl.ds(mine_planes, planes)], own_sem.at[2]),
        pltpu.make_async_copy(
            psi_early.at[:, :, mine, :], psi.at[1, :, pl.ds(mine_planes, planes)], own_sem.at[3]),
        pltpu.make_async_copy(controls, ctl, own_sem.at[4]),
    ]
    for copy in own:
        copy.start()

    barrier = pltpu.get_barrier_semaphore()
    here = 2 * g + c

    def greet(d, _):
        there = lax.rem(here + d, group)
        pl.semaphore_signal(
            barrier, inc=1, device_id=(start, there // 2, lax.rem(there, 2)), device_id_type=MESH)
        return 0

    lax.fori_loop(1, group, greet, 0)
    pl.semaphore_wait(barrier, group - 1)

    theirs = pl.ds(other_at, half)

    def trade(src, dst, i):
        return remote(src, dst, t_send.at[i], t_recv.at[i], partner, c)

    def trades(at, flag):
        rim = flag * (planes - 1)
        rest = pl.ds(1 - flag, planes - 1)
        rest_to = pl.ds(at + 2 - flag, planes - 1)
        moves = [
            trade(chi.at[:, rim, theirs, :], field.at[0, :, 1 + at + rim], 0),
            trade(chi.at[:, rest, theirs, :], field.at[0, :, rest_to], 1),
        ]
        for j in range(planes):
            moves.append(trade(psi_late.at[:, j, theirs, :], psi.at[0, :, at + j], 2 + 3 * j))
            moves.append(trade(trap.at[j, theirs, :], pot.at[at + j], 3 + 3 * j))
            moves.append(trade(psi_early.at[:, j, theirs, :], psi.at[1, :, at + j], 4 + 3 * j))
        return moves

    sent = trades(mine_planes, x)
    arriving = trades(other_planes, 1 - x)
    sent[0].start()
    sent[1].start()
    for j in range(planes):
        sent[2 + 3 * j].start()
        sent[3 + 3 * j].start()

    stages = field.shape[0]
    blank = jnp.zeros((half, depth), jnp.float32)

    @pl.when(jnp.logical_not(has_low))
    def _():
        for s in range(stages):
            field[s, 0, 0] = blank
            field[s, 1, 0] = blank

    @pl.when(jnp.logical_not(has_high))
    def _():
        for s in range(stages):
            field[s, 0, deep + 1] = blank
            field[s, 1, deep + 1] = blank

    @pl.when(x == 0)
    def _():
        for s in range(stages):
            edge_in[s, upper] = jnp.zeros((2, deep, depth), jnp.float32)
            rim_in[s, upper] = jnp.zeros((8, depth), jnp.float32)

    def low_copy(s, part):
        return remote(field.at[s, part, 1], field.at[s, part, deep + 1],
                      x_send.at[s, 0, part], x_recv.at[s, 1, part], g - 2, c)

    def high_copy(s, part):
        return remote(field.at[s, part, deep], field.at[s, part, 0],
                      x_send.at[s, 1, part], x_recv.at[s, 0, part], g + 2, c)

    boxes = ((edge_out, edge_in), (rim_out, rim_in))

    def pair_copy(s, box):
        source, target = boxes[box]
        return remote(source.at[s, 1 - upper], target.at[s, upper],
                      y_send.at[s, box, 0], y_recv.at[s, box, 0], partner, c)

    def core_copy(s, box):
        source, target = boxes[box]
        return remote(source.at[s, upper], target.at[s, 1 - upper],
                      y_send.at[s, box, 1], y_recv.at[s, box, 1], g, 1 - c)

    def pair_arrival(s, box):
        source, target = boxes[box]
        return remote(source.at[s, 1 - upper], target.at[s, 1 - upper],
                      y_send.at[s, box, 0], y_recv.at[s, box, 0], partner, c)

    def core_arrival(s, box):
        source, target = boxes[box]
        return remote(source.at[s, upper], target.at[s, upper],
                      y_send.at[s, box, 1], y_recv.at[s, box, 1], g, 1 - c)

    def send_low(s):
        @pl.when(has_low)
        def _():
            low_copy(s, 0).start()
            low_copy(s, 1).start()

    def send_high(s):
        @pl.when(has_high)
        def _():
            high_copy(s, 0).start()
            high_copy(s, 1).start()

    def send_edges(s, box):
        pair_copy(s, box).start()

        @pl.when(x == 1)
        def _():
            core_copy(s, box).start()

    def wait_edges(s, box):
        pair_arrival(s, box).wait_recv()

        @pl.when(x == 1)
        def _():
            core_arrival(s, box).wait_recv()

    def wait_low(s):
        @pl.when(has_low)
        def _():
            high_copy(s, 0).wait_recv()
            high_copy(s, 1).wait_recv()

    def wait_high(s):
        @pl.when(has_high)
        def _():
            low_copy(s, 0).wait_recv()
            low_copy(s, 1).wait_recv()

    index = (g // 2) * deep + lax.broadcasted_iota(jnp.int32, (deep, depth), 0)
    prof[...] = 1.0 + 0.5 * jnp.cos(
        (2.0 * math.pi / (sections * planes)) * index.astype(jnp.float32))
    own[4].wait()
    for k in range(2):
        part = ctl[1 - k, pl.ds(pl.multiple_of(upper * coarse, coarse), coarse), :]
        for m in range(pieces):
            piece = part[:, m * 128:(m + 1) * 128]
            fine[k, m, pl.ds(0, coarse, stride=2), :] = piece
            fine[k, m, pl.ds(1, coarse, stride=2), :] = piece

    def coefficients(k, first, count):
        control = jnp.concatenate([fine[k, m] for m in range(pieces)], axis=1)

        def body(i, _):
            j = first + i
            p = psi[k, 0, j]
            q = psi[k, 1, j]
            base = pot[j] + prof[pl.ds(j, 1), :] * control + 3.0
            p2 = p * p
            q2 = q * q
            both = base + p2 + q2
            coef[k, 0, j] = 2.0 * both + 4.0 * p2
            coef[k, 1, j] = 4.0 * (p * q)
            coef[k, 2, j] = 2.0 * both + 4.0 * q2
            return 0

        lax.fori_loop(0, count, body, 0)

    row = lax.broadcasted_iota(jnp.int32, (8, depth), 0)
    first_row, last_row = row == 0, row == 7
    lane = lax.broadcasted_iota(jnp.int32, (half, 128), 1)
    first_lane, last_lane = lane == 0, lane == 127

    def edge_row(s, side, part, at, end):
        if end is None:
            return edge_in[s, side, part, pl.ds(at - 1, 1), :]
        return rim_in[s, side, pl.ds(2 * part + end, 1), :]

    def neighbours(s, part, at, v, end):
        total = field[s, part, at - 1] + field[s, part, at + 1]
        blocks = [v[i * 8:(i + 1) * 8] for i in range(half // 8)]
        down = [edge_row(s, 0, part, at, end)] + [pltpu.roll(t, 1, 0) for t in blocks]
        up = [pltpu.roll(t, 7, 0) for t in blocks] + [edge_row(s, 1, part, at, end)]
        beside = [
            jnp.where(first_row, down[i], down[i + 1]) + jnp.where(last_row, up[i + 1], up[i])
            for i in range(half // 8)
        ]
        total = total + jnp.concatenate(beside, axis=0)
        blocks = [v[:, i * 128:(i + 1) * 128] for i in range(pieces)]
        down = [0.0] + [pltpu.roll(t, 1, 1) for t in blocks]
        up = [pltpu.roll(t, 127, 1) for t in blocks] + [0.0]
        beside = [
            jnp.where(first_lane, down[i], down[i + 1]) + jnp.where(last_lane, up[i + 1], up[i])
            for i in range(pieces)
        ]
        return total + jnp.concatenate(beside, axis=1)

    def term(s, at, end):
        k, n = s // 4, s % 4
        a = field[s, 0, at]
        b = field[s, 1, at]
        diag_a, mixed, diag_b = coef[k, 0, at - 1], coef[k, 1, at - 1], coef[k, 2, at - 1]
        up = diag_a * a + mixed * b - neighbours(s, 0, at, a, end)
        low = mixed * a + diag_b * b - neighbours(s, 1, at, b, end)
        scale = 0.5 * STEP_SIZE / (n + 1)
        a, b = low * -scale, up * scale
        if n == 3:
            for m in (3, 2, 1, 0):
                a += field[4 * k + m, 0, at]
                b += field[4 * k + m, 1, at]
        return a, b

    def put_edges(s, at, a, b, end):
        for part, v in ((0, a), (1, b)):
            if end is None:
                edge_out[s, 0, part, pl.ds(at - 1, 1), :] = v[0:1]
                edge_out[s, 1, part, pl.ds(at - 1, 1), :] = v[half - 1:half]
            else:
                rim_out[s, 0, pl.ds(2 * part + end, 1), :] = v[0:1]
                rim_out[s, 1, pl.ds(2 * part + end, 1), :] = v[half - 1:half]

    def overlap(k, at, a, b):
        weight = prof[pl.ds(at - 1, 1), :]
        return weight * (a * psi[k, 1, at - 1] - b * psi[k, 0, at - 1])

    def update(s, at, acc, end=None):
        a, b = term(s, at, end)
        field[s + 1, 0, at] = a
        field[s + 1, 1, at] = b
        put_edges(s + 1, at, a, b, end)
        if s == 3:
            acc = acc + overlap(0, at, a, b)
        return acc

    def fold(acc):
        for m in range(pieces):
            folded[m] = acc[:, m * 128:(m + 1) * 128]
        return jnp.concatenate(
            [folded[m, pl.ds(0, coarse, stride=2), :] + folded[m, pl.ds(1, coarse, stride=2), :]
             for m in range(pieces)], axis=1)

    own[0].wait()
    own[1].wait()
    own[2].wait()
    coefficients(0, mine_planes, planes)
    arriving[0].wait_recv()
    send_low(0)
    send_high(0)
    put_edges(0, 1, field[0, 0, 1], field[0, 1, 1], 0)
    put_edges(0, deep, field[0, 0, deep], field[0, 1, deep], 1)
    send_edges(0, 1)
    arriving[1].wait_recv()

    def first_edges(at, _):
        put_edges(0, at, field[0, 0, at], field[0, 1, at], None)
        return 0

    lax.fori_loop(2, deep, first_edges, 0)
    send_edges(0, 0)
    for j in range(planes):
        arriving[2 + 3 * j].wait_recv()
        arriving[3 + 3 * j].wait_recv()
        coefficients(0, other_planes + j, 1)
    sent[4].start()
    sent[7].start()

    late_sends = lambda d: remote(
        late_rows.at[g], late_rows.at[g], l_send.at[d], l_recv.at[g], lax.rem(g + d, sections), c)
    late_arrival = lambda d: remote(
        late_rows.at[g], late_rows.at[lax.rem(g + d, sections)], l_send.at[d],
        l_recv.at[lax.rem(g + d, sections)], lax.rem(g + d, sections), c)

    def loop(count, action):
        def body(d, _):
            action(d)
            return 0

        lax.fori_loop(1, count, body, 0)

    for s in range(stages - 1):
        acc = blank if s == 3 else 0
        wait_edges(s, 0)

        def two(i, acc, s=s):
            acc = update(s, 2 + 2 * i, acc)
            return update(s, 3 + 2 * i, acc)

        acc = lax.fori_loop(0, planes - 1, two, acc)
        send_edges(s + 1, 0)
        wait_edges(s, 1)
        wait_low(s)
        acc = update(s, 1, acc, 0)
        send_low(s + 1)
        wait_high(s)
        acc = update(s, deep, acc, 1)
        send_high(s + 1)
        send_edges(s + 1, 1)
        if s < planes - 2:
            sent[4 + 3 * (2 + s)].start()
        if s == 3:
            late_rows[g] = fold(acc)
            loop(sections, lambda d: late_sends(d).start())
            own[3].wait()
            coefficients(1, mine_planes, planes)
            for j in range(planes):
                arriving[4 + 3 * j].wait_recv()
            coefficients(1, other_planes, planes)

    s = stages - 1

    def give(j):
        return remote(result.at[:, other_planes + j], out.at[:, j, mine, :],
                      o_send.at[j], o_recv.at[j], partner, c)

    def give_arrival(j):
        return remote(result.at[:, other_planes + j], out.at[:, j, theirs, :],
                      o_send.at[j], o_recv.at[j], partner, c)

    def finish(at, accs, end=None):
        acc, square = accs
        a, b = term(s, at, end)
        result[0, at - 1] = a
        result[1, at - 1] = b
        return acc + overlap(1, at, a, b), square + (a * a + b * b)

    accs = (blank, blank)
    wait_edges(s, 0)
    inner_other = other_planes + x
    inner_mine = mine_planes + 1 - x

    def finish_send(i, accs):
        accs = finish(inner_other + i + 1, accs)
        give(x + i).start()
        return accs

    accs = lax.fori_loop(0, planes - 1, finish_send, accs)
    accs = lax.fori_loop(0, planes - 1, lambda i, t: finish(inner_mine + i + 1, t), accs)
    wait_edges(s, 1)
    wait_low(s)
    wait_high(s)
    accs = finish((1 - x) * (deep - 1) + 1, accs, 1 - x)
    give((1 - x) * (planes - 1)).start()
    accs = finish(x * (deep - 1) + 1, accs, x)
    keep = pltpu.make_async_copy(
        result.at[:, pl.ds(mine_planes, planes)], out.at[:, :, mine, :], own_sem.at[0])
    keep.start()
    acc, square = accs
    early_rows[g, 0:coarse] = fold(acc)
    early_rows[g, coarse:coarse + 8] = jnp.sum(square.reshape(half // 8, 8, depth), axis=0)

    def early_copy(d, slot):
        return remote(early_rows.at[g], early_rows.at[slot], e_send.at[d], e_recv.at[slot],
                      lax.rem(g + d, sections), c)

    def far_copy(d, slot):
        return remote(early_rows.at[g, pl.ds(coarse, 8)], far_power.at[slot], f_send.at[d],
                      f_recv.at[slot], lax.rem(g + d, sections), 1 - c)

    far_copy(0, g).start()
    loop(sections, lambda d: (early_copy(d, g).start(), far_copy(d, g).start()))

    loop(sections, lambda d: late_arrival(d).wait_recv())

    def total(source, parity):
        value = source[parity, 0:coarse]
        return lax.fori_loop(
            1, sections // 2, lambda i, t: t + source[2 * i + parity, 0:coarse], value)

    late = [total(late_rows, c), total(late_rows, 1 - c)]
    far_copy(0, g).wait_recv()
    loop(sections, lambda d: (
        early_copy(d, lax.rem(g + d, sections)).wait_recv(),
        far_copy(d, lax.rem(g + d, sections)).wait_recv()))

    def squares(i, t):
        near, far = t
        return near + early_rows[i, coarse:coarse + 8], far + far_power[i]

    zero = jnp.zeros((8, depth), jnp.float32)
    near, far = lax.fori_loop(0, sections, squares, (zero, zero))
    mean = jnp.sum(near + far) / float(sections * planes * 2 * rows * depth)
    power[0] = mean
    scale = jnp.sqrt(float(sections * planes) * (jnp.full((coarse, depth), mean) + 1e-06))
    early = [total(early_rows, c), total(early_rows, 1 - c)]
    for i in range(2):
        grad[0, i * coarse:(i + 1) * coarse] = early[i] / scale
        grad[1, i * coarse:(i + 1) * coarse] = late[i] / scale

    for copy in sent:
        copy.wait_send()
    for s in range(stages):
        for box in range(2):
            pair_copy(s, box).wait_send()

        @pl.when(x == 1)
        def _():
            for box in range(2):
                core_copy(s, box).wait_send()

        @pl.when(has_low)
        def _():
            for part in range(2):
                low_copy(s, part).wait_send()

        @pl.when(has_high)
        def _():
            for part in range(2):
                high_copy(s, part).wait_send()

    loop(sections, lambda d: (late_sends(d).wait_send(), early_copy(d, g).wait_send(),
                              far_copy(d, g).wait_send()))
    far_copy(0, g).wait_send()
    keep.wait()
    for j in range(planes):
        give(j).wait_send()
        give_arrival(j).wait_recv()


def on_device(chi_final, psi_late, psi_early, trap, controls):
    planes, rows, depth = chi_final.shape[1:]
    sections = lax.axis_size("gx")
    deep, half, coarse = 2 * planes, rows // 2, rows // 4
    stages = 8
    f32 = jnp.float32
    anywhere = pl.BlockSpec(memory_space=pltpu.HBM)
    dma = pltpu.SemaphoreType.DMA
    return pl.pallas_call(
        functools.partial(kernel, sections, planes, rows),
        out_shape=(
            jax.ShapeDtypeStruct(chi_final.shape, f32),
            jax.ShapeDtypeStruct(controls.shape, f32),
            jax.ShapeDtypeStruct((1,), f32),
        ),
        in_specs=[anywhere] * 5,
        out_specs=(
            anywhere,
            pl.BlockSpec(memory_space=pltpu.VMEM),
            pl.BlockSpec(memory_space=pltpu.SMEM),
        ),
        scratch_shapes=[
            pltpu.VMEM((stages, 2, deep + 2, half, depth), f32),
            pltpu.VMEM((2, 2, deep, half, depth), f32),
            pltpu.VMEM((deep, half, depth), f32),
            pltpu.VMEM((2, 3, deep, half, depth), f32),
            pltpu.VMEM((stages, 2, 2, deep, depth), f32),
            pltpu.VMEM((stages, 2, 2, deep, depth), f32),
            pltpu.VMEM((stages, 2, 8, depth), f32),
            pltpu.VMEM((stages, 2, 8, depth), f32),
            pltpu.VMEM((2, deep, half, depth), f32),
            pltpu.VMEM((2, depth // 128, half, 128), f32),
            pltpu.VMEM(controls.shape, f32),
            pltpu.VMEM((deep, depth), f32),
            pltpu.VMEM((depth // 128, half, 128), f32),
            pltpu.VMEM((sections, coarse, depth), f32),
            pltpu.VMEM((sections, coarse + 8, depth), f32),
            pltpu.VMEM((sections, 8, depth), f32),
            dma((stages, 2, 2)), dma((stages, 2, 2)), dma((stages, 2, 2)), dma((stages, 2, 2)),
            dma((2 + 3 * planes,)), dma((2 + 3 * planes,)), dma((5,)), dma((planes,)), dma((planes,)),
            dma((sections,)), dma((sections,)), dma((sections,)), dma((sections,)),
            dma((sections,)), dma((sections,)),
        ],
        compiler_params=pltpu.CompilerParams(
            collective_id=0, has_side_effects=True, vmem_limit_bytes=63 * 1024 * 1024
        ),
        cost_estimate=pl.CostEstimate(
            flops=400 * planes * rows * depth, bytes_accessed=3_000_000, transcendentals=0),
    )(chi_final, psi_late, psi_early, trap, controls)


def solution(mesh):
    placed = (
        P(None, ("starts", "gx"), "gy", None),
        P(None, ("starts", "gx"), "gy", None),
        P(None, ("starts", "gx"), "gy", None),
        P("gx", "gy", None),
        P("starts", "gy", None),
    )
    return jax.shard_map(
        on_device,
        mesh=mesh,
        in_specs=placed,
        out_specs=(P(None, ("starts", "gx"), "gy", None), P("starts", "gy", None), P("starts")),
        check_vma=False,
    )
```

```python
import functools
import math

import jax
import jax.numpy as jnp
from jax import lax
from jax.experimental import pallas as pl
from jax.experimental.pallas import tpu as pltpu
from jax.sharding import PartitionSpec as P

STEP_SIZE = 0.2
MESH = pl.DeviceIdType.MESH


def kernel(
    sections, planes, rows, chi, psi_late, psi_early, trap, controls,
    out, grad, power,
    field, psi, pot, coef, edge_in, edge_out, rim_in, rim_out, result, fine, ctl, prof, folded,
    late_rows, early_rows, far_power,
    x_send, x_recv, y_send, y_recv, t_send, t_recv, own_sem, o_send, o_recv,
    l_send, l_recv, e_send, e_recv, f_send, f_recv,
):
    deep, half, coarse = 2 * planes, rows // 2, rows // 4
    depth = chi.shape[3]
    pieces = depth // 128
    group = 2 * sections
    start = lax.axis_index("starts")
    g = lax.axis_index("gx")
    c = lax.axis_index("gy")
    x = lax.rem(g, 2)
    upper = lax.rem(x + c, 2)
    partner = g + 1 - 2 * x
    mine_at = pl.multiple_of(upper * half, half)
    other_at = pl.multiple_of((1 - upper) * half, half)
    mine_planes = x * planes
    other_planes = (1 - x) * planes
    has_low = g >= 2
    has_high = g < sections - 2

    def remote(src, dst, send, recv, to_g, to_c):
        return pltpu.make_async_remote_copy(
            src_ref=src, dst_ref=dst, send_sem=send, recv_sem=recv,
            device_id=(start, to_g, to_c), device_id_type=MESH,
        )

    mine = pl.ds(mine_at, half)
    own = [
        pltpu.make_async_copy(
            chi.at[:, :, mine, :], field.at[0, :, pl.ds(1 + mine_planes, planes)], own_sem.at[0]),
        pltpu.make_async_copy(
            psi_late.at[:, :, mine, :], psi.at[0, :, pl.ds(mine_planes, planes)], own_sem.at[1]),
        pltpu.make_async_copy(
            trap.at[:, mine, :], pot.at[pl.ds(mine_planes, planes)], own_sem.at[2]),
        pltpu.make_async_copy(
            psi_early.at[:, :, mine, :], psi.at[1, :, pl.ds(mine_planes, planes)], own_sem.at[3]),
        pltpu.make_async_copy(controls, ctl, own_sem.at[4]),
    ]
    for copy in own:
        copy.start()

    barrier = pltpu.get_barrier_semaphore()
    here = 2 * g + c

    def greet(d, _):
        there = lax.rem(here + d, group)
        pl.semaphore_signal(
            barrier, inc=1, device_id=(start, there // 2, lax.rem(there, 2)), device_id_type=MESH)
        return 0

    lax.fori_loop(1, group, greet, 0)
    pl.semaphore_wait(barrier, group - 1)

    theirs = pl.ds(other_at, half)

    def trade(src, dst, i):
        return remote(src, dst, t_send.at[i], t_recv.at[i], partner, c)

    def trades(at, flag):
        moves = []
        for i in range(planes):
            j = i + flag * (planes - 1 - 2 * i)
            moves.append([
                trade(chi.at[:, j, theirs, :], field.at[0, :, 1 + at + j], 4 * i),
                trade(psi_late.at[:, j, theirs, :], psi.at[0, :, at + j], 4 * i + 1),
                trade(trap.at[j, theirs, :], pot.at[at + j], 4 * i + 2),
                trade(psi_early.at[:, j, theirs, :], psi.at[1, :, at + j], 4 * i + 3),
            ])
        return moves

    sent = trades(mine_planes, x)
    arriving = trades(other_planes, 1 - x)
    sent[0][0].start()
    sent[1][0].start()
    sent[0][1].start()
    sent[0][2].start()
    for i in range(2, planes):
        sent[i][0].start()
    for i in range(1, planes):
        sent[i][1].start()
        sent[i][2].start()

    stages = field.shape[0]
    blank = jnp.zeros((half, depth), jnp.float32)

    @pl.when(jnp.logical_not(has_low))
    def _():
        for s in range(stages):
            field[s, 0, 0] = blank
            field[s, 1, 0] = blank

    @pl.when(jnp.logical_not(has_high))
    def _():
        for s in range(stages):
            field[s, 0, deep + 1] = blank
            field[s, 1, deep + 1] = blank

    @pl.when(x == 0)
    def _():
        for s in range(stages):
            edge_in[s, upper] = jnp.zeros((2, deep, depth), jnp.float32)
            rim_in[s, upper] = jnp.zeros((8, depth), jnp.float32)

    def low_copy(s, part):
        return remote(field.at[s, part, 1], field.at[s, part, deep + 1],
                      x_send.at[s, 0, part], x_recv.at[s, 1, part], g - 2, c)

    def high_copy(s, part):
        return remote(field.at[s, part, deep], field.at[s, part, 0],
                      x_send.at[s, 1, part], x_recv.at[s, 0, part], g + 2, c)

    boxes = ((edge_out, edge_in), (rim_out, rim_in))

    def pair_copy(s, box):
        source, target = boxes[box]
        return remote(source.at[s, 1 - upper], target.at[s, upper],
                      y_send.at[s, box, 0], y_recv.at[s, box, 0], partner, c)

    def core_copy(s, box):
        source, target = boxes[box]
        return remote(source.at[s, upper], target.at[s, 1 - upper],
                      y_send.at[s, box, 1], y_recv.at[s, box, 1], g, 1 - c)

    def pair_arrival(s, box):
        source, target = boxes[box]
        return remote(source.at[s, 1 - upper], target.at[s, 1 - upper],
                      y_send.at[s, box, 0], y_recv.at[s, box, 0], partner, c)

    def core_arrival(s, box):
        source, target = boxes[box]
        return remote(source.at[s, upper], target.at[s, upper],
                      y_send.at[s, box, 1], y_recv.at[s, box, 1], g, 1 - c)

    def send_low(s):
        @pl.when(has_low)
        def _():
            low_copy(s, 0).start()
            low_copy(s, 1).start()

    def send_high(s):
        @pl.when(has_high)
        def _():
            high_copy(s, 0).start()
            high_copy(s, 1).start()

    def send_edges(s, box):
        pair_copy(s, box).start()

        @pl.when(x == 1)
        def _():
            core_copy(s, box).start()

    def wait_edges(s, box):
        pair_arrival(s, box).wait_recv()

        @pl.when(x == 1)
        def _():
            core_arrival(s, box).wait_recv()

    def wait_low(s):
        @pl.when(has_low)
        def _():
            high_copy(s, 0).wait_recv()
            high_copy(s, 1).wait_recv()

    def wait_high(s):
        @pl.when(has_high)
        def _():
            low_copy(s, 0).wait_recv()
            low_copy(s, 1).wait_recv()

    index = (g // 2) * deep + lax.broadcasted_iota(jnp.int32, (deep, depth), 0)
    prof[...] = 1.0 + 0.5 * jnp.cos(
        (2.0 * math.pi / (sections * planes)) * index.astype(jnp.float32))
    own[4].wait()
    for k in range(2):
        part = ctl[1 - k, pl.ds(pl.multiple_of(upper * coarse, coarse), coarse), :]
        for m in range(pieces):
            piece = part[:, m * 128:(m + 1) * 128]
            fine[k, m, pl.ds(0, coarse, stride=2), :] = piece
            fine[k, m, pl.ds(1, coarse, stride=2), :] = piece

    def coefficients(k, first, count):
        control = jnp.concatenate([fine[k, m] for m in range(pieces)], axis=1)

        def body(i, _):
            j = first + i
            p = psi[k, 0, j]
            q = psi[k, 1, j]
            base = pot[j] + prof[pl.ds(j, 1), :] * control + 3.0
            p2 = p * p
            q2 = q * q
            both = base + p2 + q2
            coef[k, 0, j] = 2.0 * both + 4.0 * p2
            coef[k, 1, j] = 4.0 * (p * q)
            coef[k, 2, j] = 2.0 * both + 4.0 * q2
            return 0

        lax.fori_loop(0, count, body, 0)

    row = lax.broadcasted_iota(jnp.int32, (8, depth), 0)
    first_row, last_row = row == 0, row == 7
    lane = lax.broadcasted_iota(jnp.int32, (half, 128), 1)
    first_lane, last_lane = lane == 0, lane == 127

    def edge_row(s, side, part, at, end):
        if end is None:
            return edge_in[s, side, part, pl.ds(at - 1, 1), :]
        return rim_in[s, side, pl.ds(2 * part + end, 1), :]

    def neighbours(s, part, at, v, end):
        total = field[s, part, at - 1] + field[s, part, at + 1]
        blocks = [v[i * 8:(i + 1) * 8] for i in range(half // 8)]
        down = [edge_row(s, 0, part, at, end)] + [pltpu.roll(t, 1, 0) for t in blocks]
        up = [pltpu.roll(t, 7, 0) for t in blocks] + [edge_row(s, 1, part, at, end)]
        beside = [
            jnp.where(first_row, down[i], down[i + 1]) + jnp.where(last_row, up[i + 1], up[i])
            for i in range(half // 8)
        ]
        total = total + jnp.concatenate(beside, axis=0)
        blocks = [v[:, i * 128:(i + 1) * 128] for i in range(pieces)]
        down = [0.0] + [pltpu.roll(t, 1, 1) for t in blocks]
        up = [pltpu.roll(t, 127, 1) for t in blocks] + [0.0]
        beside = [
            jnp.where(first_lane, down[i], down[i + 1]) + jnp.where(last_lane, up[i + 1], up[i])
            for i in range(pieces)
        ]
        return total + jnp.concatenate(beside, axis=1)

    def term(s, at, end):
        k, n = s // 4, s % 4
        a = field[s, 0, at]
        b = field[s, 1, at]
        diag_a, mixed, diag_b = coef[k, 0, at - 1], coef[k, 1, at - 1], coef[k, 2, at - 1]
        up = diag_a * a + mixed * b - neighbours(s, 0, at, a, end)
        low = mixed * a + diag_b * b - neighbours(s, 1, at, b, end)
        scale = 0.5 * STEP_SIZE / (n + 1)
        a, b = low * -scale, up * scale
        if n == 3:
            for m in (3, 2, 1, 0):
                a += field[4 * k + m, 0, at]
                b += field[4 * k + m, 1, at]
        return a, b

    def put_edges(s, at, a, b, end):
        for part, v in ((0, a), (1, b)):
            if end is None:
                edge_out[s, 0, part, pl.ds(at - 1, 1), :] = v[0:1]
                edge_out[s, 1, part, pl.ds(at - 1, 1), :] = v[half - 1:half]
            else:
                rim_out[s, 0, pl.ds(2 * part + end, 1), :] = v[0:1]
                rim_out[s, 1, pl.ds(2 * part + end, 1), :] = v[half - 1:half]

    def overlap(k, at, a, b):
        weight = prof[pl.ds(at - 1, 1), :]
        return weight * (a * psi[k, 1, at - 1] - b * psi[k, 0, at - 1])

    def update(s, at, acc, end=None):
        a, b = term(s, at, end)
        field[s + 1, 0, at] = a
        field[s + 1, 1, at] = b
        put_edges(s + 1, at, a, b, end)
        if s == 3:
            acc = acc + overlap(0, at, a, b)
        return acc

    def fold(acc):
        for m in range(pieces):
            folded[m] = acc[:, m * 128:(m + 1) * 128]
        return jnp.concatenate(
            [folded[m, pl.ds(0, coarse, stride=2), :] + folded[m, pl.ds(1, coarse, stride=2), :]
             for m in range(pieces)], axis=1)

    own[0].wait()
    own[1].wait()
    own[2].wait()
    coefficients(0, mine_planes, planes)
    arriving[0][0].wait_recv()
    send_low(0)
    send_high(0)
    put_edges(0, 1, field[0, 0, 1], field[0, 1, 1], 0)
    put_edges(0, deep, field[0, 0, deep], field[0, 1, deep], 1)
    send_edges(0, 1)
    arriving[1][0].wait_recv()
    arriving[0][1].wait_recv()
    arriving[0][2].wait_recv()
    coefficients(0, (1 - x) * (deep - 1), 1)

    def first_edges(at, _):
        put_edges(0, at, field[0, 0, at], field[0, 1, at], None)
        return 0

    late_sends = lambda d: remote(
        late_rows.at[g], late_rows.at[g], l_send.at[d], l_recv.at[g], lax.rem(g + d, sections), c)
    late_arrival = lambda d: remote(
        late_rows.at[g], late_rows.at[lax.rem(g + d, sections)], l_send.at[d],
        l_recv.at[lax.rem(g + d, sections)], lax.rem(g + d, sections), c)

    def loop(count, action):
        def body(d, _):
            action(d)
            return 0

        lax.fori_loop(1, count, body, 0)

    for s in range(stages - 1):
        acc = blank if s == 3 else 0
        wait_edges(s, 1)
        wait_low(s)
        acc = update(s, 1, acc, 0)
        send_low(s + 1)
        wait_high(s)
        acc = update(s, deep, acc, 1)
        send_high(s + 1)
        send_edges(s + 1, 1)
        if s == 0:
            for i in range(2, planes):
                arriving[i][0].wait_recv()
            lax.fori_loop(2, deep, first_edges, 0)
            send_edges(0, 0)
            for i in range(1, planes):
                arriving[i][1].wait_recv()
                arriving[i][2].wait_recv()
                coefficients(0, (1 - x) * (deep - 1) + i * (2 * x - 1), 1)
            sent[0][3].start()
            sent[1][3].start()
        wait_edges(s, 0)

        def two(i, acc, s=s):
            acc = update(s, 2 + 2 * i, acc)
            return update(s, 3 + 2 * i, acc)

        acc = lax.fori_loop(0, planes - 1, two, acc)
        send_edges(s + 1, 0)
        if 1 <= s < planes - 1:
            sent[s + 1][3].start()
        if s == 3:
            late_rows[g] = fold(acc)
            loop(sections, lambda d: late_sends(d).start())
            own[3].wait()
            coefficients(1, mine_planes, planes)
            for j in range(planes):
                arriving[j][3].wait_recv()
            coefficients(1, other_planes, planes)

    s = stages - 1

    def give(j):
        return remote(result.at[:, other_planes + j], out.at[:, j, mine, :],
                      o_send.at[j], o_recv.at[j], partner, c)

    def give_arrival(j):
        return remote(result.at[:, other_planes + j], out.at[:, j, theirs, :],
                      o_send.at[j], o_recv.at[j], partner, c)

    def finish(at, accs, end=None):
        acc, square = accs
        a, b = term(s, at, end)
        result[0, at - 1] = a
        result[1, at - 1] = b
        return acc + overlap(1, at, a, b), square + (a * a + b * b)

    accs = (blank, blank)
    wait_edges(s, 0)
    inner_other = other_planes + x
    inner_mine = mine_planes + 1 - x

    def finish_send(i, accs):
        accs = finish(inner_other + i + 1, accs)
        give(x + i).start()
        return accs

    accs = lax.fori_loop(0, planes - 1, finish_send, accs)
    accs = lax.fori_loop(0, planes - 1, lambda i, t: finish(inner_mine + i + 1, t), accs)
    wait_edges(s, 1)
    wait_low(s)
    wait_high(s)
    accs = finish((1 - x) * (deep - 1) + 1, accs, 1 - x)
    give((1 - x) * (planes - 1)).start()
    accs = finish(x * (deep - 1) + 1, accs, x)
    keep = pltpu.make_async_copy(
        result.at[:, pl.ds(mine_planes, planes)], out.at[:, :, mine, :], own_sem.at[0])
    keep.start()
    acc, square = accs
    early_rows[g, 0:coarse] = fold(acc)
    early_rows[g, coarse:coarse + 8] = jnp.sum(square.reshape(half // 8, 8, depth), axis=0)

    def early_copy(d, slot):
        return remote(early_rows.at[g], early_rows.at[slot], e_send.at[d], e_recv.at[slot],
                      lax.rem(g + d, sections), c)

    def far_copy(d, slot):
        return remote(early_rows.at[g, pl.ds(coarse, 8)], far_power.at[slot], f_send.at[d],
                      f_recv.at[slot], lax.rem(g + d, sections), 1 - c)

    far_copy(0, g).start()
    loop(sections, lambda d: (early_copy(d, g).start(), far_copy(d, g).start()))

    loop(sections, lambda d: late_arrival(d).wait_recv())

    def total(source, parity):
        value = source[parity, 0:coarse]
        return lax.fori_loop(
            1, sections // 2, lambda i, t: t + source[2 * i + parity, 0:coarse], value)

    late = [total(late_rows, c), total(late_rows, 1 - c)]
    far_copy(0, g).wait_recv()
    loop(sections, lambda d: (
        early_copy(d, lax.rem(g + d, sections)).wait_recv(),
        far_copy(d, lax.rem(g + d, sections)).wait_recv()))

    def squares(i, t):
        near, far = t
        return near + early_rows[i, coarse:coarse + 8], far + far_power[i]

    zero = jnp.zeros((8, depth), jnp.float32)
    near, far = lax.fori_loop(0, sections, squares, (zero, zero))
    mean = jnp.sum(near + far) / float(sections * planes * 2 * rows * depth)
    power[0] = mean
    scale = jnp.sqrt(float(sections * planes) * (jnp.full((coarse, depth), mean) + 1e-06))
    early = [total(early_rows, c), total(early_rows, 1 - c)]
    for i in range(2):
        grad[0, i * coarse:(i + 1) * coarse] = early[i] / scale
        grad[1, i * coarse:(i + 1) * coarse] = late[i] / scale

    for moves in sent:
        for copy in moves:
            copy.wait_send()
    for s in range(stages):
        for box in range(2):
            pair_copy(s, box).wait_send()

        @pl.when(x == 1)
        def _():
            for box in range(2):
                core_copy(s, box).wait_send()

        @pl.when(has_low)
        def _():
            for part in range(2):
                low_copy(s, part).wait_send()

        @pl.when(has_high)
        def _():
            for part in range(2):
                high_copy(s, part).wait_send()

    loop(sections, lambda d: (late_sends(d).wait_send(), early_copy(d, g).wait_send(),
                              far_copy(d, g).wait_send()))
    far_copy(0, g).wait_send()
    keep.wait()
    for j in range(planes):
        give(j).wait_send()
        give_arrival(j).wait_recv()


def finish_kernel(field_in, grad_in, field_out, grad_out, sems):
    planes = field_in.shape[1]
    copies = [pltpu.make_async_copy(grad_in, grad_out, sems.at[2 * planes])]
    for part in range(2):
        for j in range(planes):
            copies.append(pltpu.make_async_copy(
                field_in.at[part, j], field_out.at[part, j], sems.at[part * planes + j]))
    for copy in copies:
        copy.start()
    for copy in copies:
        copy.wait()


def on_device(chi_final, psi_late, psi_early, trap, controls):
    planes, rows, depth = chi_final.shape[1:]
    sections = lax.axis_size("gx")
    deep, half, coarse = 2 * planes, rows // 2, rows // 4
    stages = 8
    f32 = jnp.float32
    anywhere = pl.BlockSpec(memory_space=pltpu.HBM)
    dma = pltpu.SemaphoreType.DMA
    chi_start, grad_rows, power = pl.pallas_call(
        functools.partial(kernel, sections, planes, rows),
        out_shape=(
            jax.ShapeDtypeStruct(chi_final.shape, f32),
            jax.ShapeDtypeStruct(controls.shape, f32),
            jax.ShapeDtypeStruct((1,), f32),
        ),
        in_specs=[anywhere] * 5,
        out_specs=(
            anywhere,
            pl.BlockSpec(memory_space=pltpu.VMEM),
            pl.BlockSpec(memory_space=pltpu.SMEM),
        ),
        scratch_shapes=[
            pltpu.VMEM((stages, 2, deep + 2, half, depth), f32),
            pltpu.VMEM((2, 2, deep, half, depth), f32),
            pltpu.VMEM((deep, half, depth), f32),
            pltpu.VMEM((2, 3, deep, half, depth), f32),
            pltpu.VMEM((stages, 2, 2, deep, depth), f32),
            pltpu.VMEM((stages, 2, 2, deep, depth), f32),
            pltpu.VMEM((stages, 2, 8, depth), f32),
            pltpu.VMEM((stages, 2, 8, depth), f32),
            pltpu.VMEM((2, deep, half, depth), f32),
            pltpu.VMEM((2, depth // 128, half, 128), f32),
            pltpu.VMEM(controls.shape, f32),
            pltpu.VMEM((deep, depth), f32),
            pltpu.VMEM((depth // 128, half, 128), f32),
            pltpu.VMEM((sections, coarse, depth), f32),
            pltpu.VMEM((sections, coarse + 8, depth), f32),
            pltpu.VMEM((sections, 8, depth), f32),
            dma((stages, 2, 2)), dma((stages, 2, 2)), dma((stages, 2, 2)), dma((stages, 2, 2)),
            dma((4 * planes,)), dma((4 * planes,)), dma((5,)), dma((planes,)), dma((planes,)),
            dma((sections,)), dma((sections,)), dma((sections,)), dma((sections,)),
            dma((sections,)), dma((sections,)),
        ],
        compiler_params=pltpu.CompilerParams(
            collective_id=0, has_side_effects=True, vmem_limit_bytes=63 * 1024 * 1024
        ),
        cost_estimate=pl.CostEstimate(
            flops=400 * planes * rows * depth, bytes_accessed=3_000_000, transcendentals=0),
    )(chi_final, psi_late, psi_early, trap, controls)
    chi_start, grad_rows = pl.pallas_call(
        finish_kernel,
        out_shape=(
            jax.ShapeDtypeStruct(chi_final.shape, f32),
            jax.ShapeDtypeStruct(controls.shape, f32),
        ),
        in_specs=[anywhere] * 2,
        out_specs=(anywhere, anywhere),
        scratch_shapes=[dma((2 * planes + 1,))],
        compiler_params=pltpu.CompilerParams(vmem_limit_bytes=63 * 1024 * 1024),
    )(chi_start, grad_rows)
    return chi_start, grad_rows, power


def solution(mesh):
    placed = (
        P(None, ("starts", "gx"), "gy", None),
        P(None, ("starts", "gx"), "gy", None),
        P(None, ("starts", "gx"), "gy", None),
        P("gx", "gy", None),
        P("starts", "gy", None),
    )
    return jax.shard_map(
        on_device,
        mesh=mesh,
        in_specs=placed,
        out_specs=(P(None, ("starts", "gx"), "gy", None), P("starts", "gy", None), P("starts")),
        check_vma=False,
    )
```

```python
import functools
import math

import jax
import jax.numpy as jnp
from jax import lax
from jax.experimental import pallas as pl
from jax.experimental.pallas import tpu as pltpu
from jax.sharding import PartitionSpec as P

STEP_SIZE = 0.2
MESH = pl.DeviceIdType.MESH


def kernel(
    sections, planes, rows, chi, psi_late, psi_early, trap, controls,
    out, grad, power,
    field, psi, pot, coef, edge_in, edge_out, rim_in, rim_out, result, fine, ctl, prof, folded,
    late_rows, early_rows, far_power,
    x_send, x_recv, y_send, y_recv, t_send, t_recv, own_sem, o_send, o_recv,
    l_send, l_recv, e_send, e_recv, f_send, f_recv, give_chi, give_psi, give_trap, back,
):
    deep, half, coarse = 2 * planes, rows // 2, rows // 4
    depth = chi.shape[3]
    pieces = depth // 128
    group = 2 * sections
    start = lax.axis_index("starts")
    g = lax.axis_index("gx")
    c = lax.axis_index("gy")
    x = lax.rem(g, 2)
    upper = lax.rem(x + c, 2)
    partner = g + 1 - 2 * x
    mine_at = pl.multiple_of(upper * half, half)
    other_at = pl.multiple_of((1 - upper) * half, half)
    mine_planes = x * planes
    other_planes = (1 - x) * planes
    has_low = g >= 2
    has_high = g < sections - 2

    def remote(src, dst, send, recv, to_g, to_c):
        return pltpu.make_async_remote_copy(
            src_ref=src, dst_ref=dst, send_sem=send, recv_sem=recv,
            device_id=(start, to_g, to_c), device_id_type=MESH,
        )

    mine = pl.ds(mine_at, half)
    own = [
        pltpu.make_async_copy(
            chi.at[:, :, mine, :], field.at[0, :, pl.ds(1 + mine_planes, planes)], own_sem.at[0]),
        pltpu.make_async_copy(
            psi_late.at[:, :, mine, :], psi.at[0, :, pl.ds(mine_planes, planes)], own_sem.at[1]),
        pltpu.make_async_copy(
            trap.at[:, mine, :], pot.at[pl.ds(mine_planes, planes)], own_sem.at[2]),
        pltpu.make_async_copy(
            psi_early.at[:, :, mine, :], psi.at[1, :, pl.ds(mine_planes, planes)], own_sem.at[3]),
        pltpu.make_async_copy(controls, ctl, own_sem.at[4]),
    ]
    theirs = pl.ds(other_at, half)
    staged = [
        pltpu.make_async_copy(chi.at[:, :, theirs, :], give_chi, own_sem.at[5]),
        pltpu.make_async_copy(psi_late.at[:, :, theirs, :], give_psi.at[0], own_sem.at[6]),
        pltpu.make_async_copy(trap.at[:, theirs, :], give_trap, own_sem.at[7]),
        pltpu.make_async_copy(psi_early.at[:, :, theirs, :], give_psi.at[1], own_sem.at[8]),
    ]
    for copy in staged:
        copy.start()
    for copy in own:
        copy.start()

    barrier = pltpu.get_barrier_semaphore()
    here = 2 * g + c

    def greet(d, _):
        there = lax.rem(here + d, group)
        pl.semaphore_signal(
            barrier, inc=1, device_id=(start, there // 2, lax.rem(there, 2)), device_id_type=MESH)
        return 0

    lax.fori_loop(1, group, greet, 0)
    pl.semaphore_wait(barrier, group - 1)

    for copy in staged:
        copy.wait()

    def trade(src, dst, i):
        return remote(src, dst, t_send.at[i], t_recv.at[i], partner, c)

    def trades(at, flag):
        moves = []
        for i in range(planes):
            j = i + flag * (planes - 1 - 2 * i)
            moves.append([
                trade(give_chi.at[:, j], field.at[0, :, 1 + at + j], 4 * i),
                trade(give_psi.at[0, :, j], psi.at[0, :, at + j], 4 * i + 1),
                trade(give_trap.at[j], pot.at[at + j], 4 * i + 2),
                trade(give_psi.at[1, :, j], psi.at[1, :, at + j], 4 * i + 3),
            ])
        return moves

    sent = trades(mine_planes, x)
    arriving = trades(other_planes, 1 - x)
    sent[0][0].start()
    sent[1][0].start()
    sent[0][1].start()
    sent[0][2].start()
    for i in range(2, planes):
        sent[i][0].start()
    for i in range(1, planes):
        sent[i][1].start()
        sent[i][2].start()

    stages = field.shape[0]
    blank = jnp.zeros((half, depth), jnp.float32)

    @pl.when(jnp.logical_not(has_low))
    def _():
        for s in range(stages):
            field[s, 0, 0] = blank
            field[s, 1, 0] = blank

    @pl.when(jnp.logical_not(has_high))
    def _():
        for s in range(stages):
            field[s, 0, deep + 1] = blank
            field[s, 1, deep + 1] = blank

    @pl.when(x == 0)
    def _():
        for s in range(stages):
            edge_in[s, upper] = jnp.zeros((2, deep, depth), jnp.float32)
            rim_in[s, upper] = jnp.zeros((8, depth), jnp.float32)

    def low_copy(s):
        return remote(field.at[s, :, 1], field.at[s, :, deep + 1],
                      x_send.at[s, 0], x_recv.at[s, 1], g - 2, c)

    def high_copy(s):
        return remote(field.at[s, :, deep], field.at[s, :, 0],
                      x_send.at[s, 1], x_recv.at[s, 0], g + 2, c)

    boxes = ((edge_out, edge_in), (rim_out, rim_in))

    def pair_copy(s, box):
        source, target = boxes[box]
        return remote(source.at[s, 1 - upper], target.at[s, upper],
                      y_send.at[s, box, 0], y_recv.at[s, box, 0], partner, c)

    def core_copy(s, box):
        source, target = boxes[box]
        return remote(source.at[s, upper], target.at[s, 1 - upper],
                      y_send.at[s, box, 1], y_recv.at[s, box, 1], g, 1 - c)

    def pair_arrival(s, box):
        source, target = boxes[box]
        return remote(source.at[s, 1 - upper], target.at[s, 1 - upper],
                      y_send.at[s, box, 0], y_recv.at[s, box, 0], partner, c)

    def core_arrival(s, box):
        source, target = boxes[box]
        return remote(source.at[s, upper], target.at[s, upper],
                      y_send.at[s, box, 1], y_recv.at[s, box, 1], g, 1 - c)

    def send_low(s):
        @pl.when(has_low)
        def _():
            low_copy(s).start()

    def send_high(s):
        @pl.when(has_high)
        def _():
            high_copy(s).start()

    def send_edges(s, box):
        pair_copy(s, box).start()

        @pl.when(x == 1)
        def _():
            core_copy(s, box).start()

    def wait_edges(s, box):
        pair_arrival(s, box).wait_recv()

        @pl.when(x == 1)
        def _():
            core_arrival(s, box).wait_recv()

    def wait_low(s):
        @pl.when(has_low)
        def _():
            high_copy(s).wait_recv()

    def wait_high(s):
        @pl.when(has_high)
        def _():
            low_copy(s).wait_recv()

    def settle(s):
        for box in range(2):
            pair_copy(s, box).wait_send()

        @pl.when(x == 1)
        def _():
            for box in range(2):
                core_copy(s, box).wait_send()

        @pl.when(has_low)
        def _():
            low_copy(s).wait_send()

        @pl.when(has_high)
        def _():
            high_copy(s).wait_send()

    index = (g // 2) * deep + lax.broadcasted_iota(jnp.int32, (deep, depth), 0)
    prof[...] = 1.0 + 0.5 * jnp.cos(
        (2.0 * math.pi / (sections * planes)) * index.astype(jnp.float32))
    own[4].wait()
    for k in range(2):
        part = ctl[1 - k, pl.ds(pl.multiple_of(upper * coarse, coarse), coarse), :]
        for m in range(pieces):
            piece = part[:, m * 128:(m + 1) * 128]
            fine[k, m, pl.ds(0, coarse, stride=2), :] = piece
            fine[k, m, pl.ds(1, coarse, stride=2), :] = piece

    def coefficients(k, first, count):
        control = jnp.concatenate([fine[k, m] for m in range(pieces)], axis=1)

        def body(i, _):
            j = first + i
            p = psi[k, 0, j]
            q = psi[k, 1, j]
            base = pot[j] + prof[pl.ds(j, 1), :] * control + 3.0
            p2 = p * p
            q2 = q * q
            both = base + p2 + q2
            coef[k, 0, j] = 2.0 * both + 4.0 * p2
            coef[k, 1, j] = 4.0 * (p * q)
            coef[k, 2, j] = 2.0 * both + 4.0 * q2
            return 0

        lax.fori_loop(0, count, body, 0)

    row = lax.broadcasted_iota(jnp.int32, (8, depth), 0)
    first_row, last_row = row == 0, row == 7
    lane = lax.broadcasted_iota(jnp.int32, (half, 128), 1)
    first_lane, last_lane = lane == 0, lane == 127

    def edge_row(s, side, part, at, end):
        if end is None:
            return edge_in[s, side, part, pl.ds(at - 1, 1), :]
        return rim_in[s, side, pl.ds(2 * part + end, 1), :]

    def neighbours(s, part, at, v, end):
        total = field[s, part, at - 1] + field[s, part, at + 1]
        blocks = [v[i * 8:(i + 1) * 8] for i in range(half // 8)]
        down = [edge_row(s, 0, part, at, end)] + [pltpu.roll(t, 1, 0) for t in blocks]
        up = [pltpu.roll(t, 7, 0) for t in blocks] + [edge_row(s, 1, part, at, end)]
        beside = [
            jnp.where(first_row, down[i], down[i + 1]) + jnp.where(last_row, up[i + 1], up[i])
            for i in range(half // 8)
        ]
        total = total + jnp.concatenate(beside, axis=0)
        blocks = [v[:, i * 128:(i + 1) * 128] for i in range(pieces)]
        down = [0.0] + [pltpu.roll(t, 1, 1) for t in blocks]
        up = [pltpu.roll(t, 127, 1) for t in blocks] + [0.0]
        beside = [
            jnp.where(first_lane, down[i], down[i + 1]) + jnp.where(last_lane, up[i + 1], up[i])
            for i in range(pieces)
        ]
        return total + jnp.concatenate(beside, axis=1)

    def term(s, at, end):
        k, n = s // 4, s % 4
        a = field[s, 0, at]
        b = field[s, 1, at]
        diag_a, mixed, diag_b = coef[k, 0, at - 1], coef[k, 1, at - 1], coef[k, 2, at - 1]
        up = diag_a * a + mixed * b - neighbours(s, 0, at, a, end)
        low = mixed * a + diag_b * b - neighbours(s, 1, at, b, end)
        scale = 0.5 * STEP_SIZE / (n + 1)
        a, b = low * -scale, up * scale
        if n == 3:
            for m in (3, 2, 1, 0):
                a += field[4 * k + m, 0, at]
                b += field[4 * k + m, 1, at]
        return a, b

    def put_edges(s, at, a, b, end):
        for part, v in ((0, a), (1, b)):
            if end is None:
                edge_out[s, 0, part, pl.ds(at - 1, 1), :] = v[0:1]
                edge_out[s, 1, part, pl.ds(at - 1, 1), :] = v[half - 1:half]
            else:
                rim_out[s, 0, pl.ds(2 * part + end, 1), :] = v[0:1]
                rim_out[s, 1, pl.ds(2 * part + end, 1), :] = v[half - 1:half]

    def overlap(k, at, a, b):
        weight = prof[pl.ds(at - 1, 1), :]
        return weight * (a * psi[k, 1, at - 1] - b * psi[k, 0, at - 1])

    def update(s, at, acc, end=None):
        a, b = term(s, at, end)
        field[s + 1, 0, at] = a
        field[s + 1, 1, at] = b
        put_edges(s + 1, at, a, b, end)
        if s == 3:
            acc = acc + overlap(0, at, a, b)
        return acc

    def fold(acc):
        for m in range(pieces):
            folded[m] = acc[:, m * 128:(m + 1) * 128]
        return jnp.concatenate(
            [folded[m, pl.ds(0, coarse, stride=2), :] + folded[m, pl.ds(1, coarse, stride=2), :]
             for m in range(pieces)], axis=1)

    own[0].wait()
    own[1].wait()
    own[2].wait()
    coefficients(0, mine_planes, planes)
    arriving[0][0].wait_recv()
    send_low(0)
    send_high(0)
    put_edges(0, 1, field[0, 0, 1], field[0, 1, 1], 0)
    put_edges(0, deep, field[0, 0, deep], field[0, 1, deep], 1)
    send_edges(0, 1)
    arriving[1][0].wait_recv()
    arriving[0][1].wait_recv()
    arriving[0][2].wait_recv()
    coefficients(0, (1 - x) * (deep - 1), 1)

    def first_edges(at, _):
        put_edges(0, at, field[0, 0, at], field[0, 1, at], None)
        return 0

    late_sends = lambda d: remote(
        late_rows.at[g], late_rows.at[g], l_send.at[d], l_recv.at[g], lax.rem(g + d, sections), c)
    late_arrival = lambda d: remote(
        late_rows.at[g], late_rows.at[lax.rem(g + d, sections)], l_send.at[d],
        l_recv.at[lax.rem(g + d, sections)], lax.rem(g + d, sections), c)

    def loop(count, action):
        def body(d, _):
            action(d)
            return 0

        lax.fori_loop(1, count, body, 0)

    def total(source, parity):
        value = source[parity, 0:coarse]
        return lax.fori_loop(
            1, sections // 2, lambda i, t: t + source[2 * i + parity, 0:coarse], value)

    for s in range(stages - 1):
        acc = blank if s == 3 else 0
        wait_edges(s, 1)
        wait_low(s)
        acc = update(s, 1, acc, 0)
        send_low(s + 1)
        wait_high(s)
        acc = update(s, deep, acc, 1)
        send_high(s + 1)
        send_edges(s + 1, 1)
        if 1 <= s < planes:
            sent[s][3].start()
        if s == 0:
            for i in range(2, planes):
                arriving[i][0].wait_recv()
            lax.fori_loop(2, deep, first_edges, 0)
            send_edges(0, 0)
            for i in range(1, planes):
                arriving[i][1].wait_recv()
                arriving[i][2].wait_recv()
                coefficients(0, (1 - x) * (deep - 1) + i * (2 * x - 1), 1)
            sent[0][3].start()
        wait_edges(s, 0)

        def two(i, acc, s=s):
            acc = update(s, 2 + 2 * i, acc)
            return update(s, 3 + 2 * i, acc)

        acc = lax.fori_loop(0, planes - 1, two, acc)
        send_edges(s + 1, 0)
        settle(s)
        if s == 4:
            for moves in sent:
                for copy in moves:
                    copy.wait_send()
        if s == 6:
            loop(sections, lambda d: late_arrival(d).wait_recv())
            loop(sections, lambda d: late_sends(d).wait_send())
            for i, parity in enumerate((c, 1 - c)):
                grad[1, i * coarse:(i + 1) * coarse] = total(late_rows, parity)
        if s == 3:
            late_rows[g] = fold(acc)
            loop(sections, lambda d: late_sends(d).start())
            own[3].wait()
            coefficients(1, mine_planes, planes)
            for j in range(planes):
                arriving[j][3].wait_recv()
            coefficients(1, other_planes, planes)

    s = stages - 1

    def give(j):
        return remote(result.at[:, other_planes + j], back.at[:, j],
                      o_send.at[j], o_recv.at[j], partner, c)

    def put_back(j):
        return pltpu.make_async_copy(back.at[:, j], out.at[:, j, theirs, :], own_sem.at[9 + j])

    def finish(at, accs, end=None):
        acc, square = accs
        a, b = term(s, at, end)
        result[0, at - 1] = a
        result[1, at - 1] = b
        return acc + overlap(1, at, a, b), square + (a * a + b * b)

    accs = (blank, blank)
    wait_edges(s, 0)
    inner_other = other_planes + x
    inner_mine = mine_planes + 1 - x

    def finish_send(i, accs):
        accs = finish(inner_other + i + 1, accs)
        give(x + i).start()
        return accs

    accs = lax.fori_loop(0, planes - 1, finish_send, accs)
    accs = lax.fori_loop(0, planes - 1, lambda i, t: finish(inner_mine + i + 1, t), accs)
    wait_edges(s, 1)
    wait_low(s)
    wait_high(s)
    accs = finish((1 - x) * (deep - 1) + 1, accs, 1 - x)
    give((1 - x) * (planes - 1)).start()
    accs = finish(x * (deep - 1) + 1, accs, x)
    keep = pltpu.make_async_copy(
        result.at[:, pl.ds(mine_planes, planes)], out.at[:, :, mine, :], own_sem.at[0])
    keep.start()
    acc, square = accs
    early_rows[g, 0:coarse] = fold(acc)
    early_rows[g, coarse:coarse + 8] = jnp.sum(square.reshape(half // 8, 8, depth), axis=0)

    def early_copy(d, slot):
        return remote(early_rows.at[g], early_rows.at[slot], e_send.at[d], e_recv.at[slot],
                      lax.rem(g + d, sections), c)

    def far_copy(d, slot):
        return remote(early_rows.at[g, pl.ds(coarse, 8)], far_power.at[slot], f_send.at[d],
                      f_recv.at[slot], lax.rem(g + d, sections), 1 - c)

    far_copy(0, g).start()
    loop(sections, lambda d: (early_copy(d, g).start(), far_copy(d, g).start()))

    settle(s)
    for j in range(planes):
        give(j).wait_send()
    for j in range(planes):
        give(j).wait_recv()
        put_back(j).start()
    far_copy(0, g).wait_recv()
    loop(sections, lambda d: (
        early_copy(d, lax.rem(g + d, sections)).wait_recv(),
        far_copy(d, lax.rem(g + d, sections)).wait_recv()))

    def squares(i, t):
        near, far = t
        return near + early_rows[i, coarse:coarse + 8], far + far_power[i]

    zero = jnp.zeros((8, depth), jnp.float32)
    near, far = lax.fori_loop(0, sections, squares, (zero, zero))
    mean = jnp.sum(near + far) / float(sections * planes * 2 * rows * depth)
    power[0] = mean
    scale = jnp.sqrt(float(sections * planes) * (jnp.full((coarse, depth), mean) + 1e-06))
    early = [total(early_rows, c), total(early_rows, 1 - c)]
    for i in range(2):
        grad[0, i * coarse:(i + 1) * coarse] = early[i] / scale
        grad[1, i * coarse:(i + 1) * coarse] = grad[1, i * coarse:(i + 1) * coarse] / scale

    loop(sections, lambda d: (early_copy(d, g).wait_send(), far_copy(d, g).wait_send()))
    far_copy(0, g).wait_send()
    keep.wait()
    for j in range(planes):
        put_back(j).wait()


def finish_kernel(field_in, grad_in, field_out, grad_out, held, held_grad, sems):
    planes = field_in.shape[1]
    moves = [(grad_in, held_grad, grad_out)]
    for part in range(2):
        for j in range(planes):
            moves.append((field_in.at[part, j], held.at[part, j], field_out.at[part, j]))
    arrive = [pltpu.make_async_copy(a, b, sems.at[0, i]) for i, (a, b, _) in enumerate(moves)]
    leave = [pltpu.make_async_copy(b, o, sems.at[1, i]) for i, (_, b, o) in enumerate(moves)]
    for copy in arrive:
        copy.start()
    for copy, then in zip(arrive, leave):
        copy.wait()
        then.start()
    for copy in leave:
        copy.wait()


def on_device(chi_final, psi_late, psi_early, trap, controls):
    planes, rows, depth = chi_final.shape[1:]
    sections = lax.axis_size("gx")
    deep, half, coarse = 2 * planes, rows // 2, rows // 4
    stages = 8
    f32 = jnp.float32
    anywhere = pl.BlockSpec(memory_space=pltpu.HBM)
    dma = pltpu.SemaphoreType.DMA
    chi_start, grad_rows, power = pl.pallas_call(
        functools.partial(kernel, sections, planes, rows),
        out_shape=(
            jax.ShapeDtypeStruct(chi_final.shape, f32),
            jax.ShapeDtypeStruct(controls.shape, f32),
            jax.ShapeDtypeStruct((1,), f32),
        ),
        in_specs=[anywhere] * 5,
        out_specs=(
            anywhere,
            pl.BlockSpec(memory_space=pltpu.VMEM),
            pl.BlockSpec(memory_space=pltpu.SMEM),
        ),
        scratch_shapes=[
            pltpu.VMEM((stages, 2, deep + 2, half, depth), f32),
            pltpu.VMEM((2, 2, deep, half, depth), f32),
            pltpu.VMEM((deep, half, depth), f32),
            pltpu.VMEM((2, 3, deep, half, depth), f32),
            pltpu.VMEM((stages, 2, 2, deep, depth), f32),
            pltpu.VMEM((stages, 2, 2, deep, depth), f32),
            pltpu.VMEM((stages, 2, 8, depth), f32),
            pltpu.VMEM((stages, 2, 8, depth), f32),
            pltpu.VMEM((2, deep, half, depth), f32),
            pltpu.VMEM((2, depth // 128, half, 128), f32),
            pltpu.VMEM(controls.shape, f32),
            pltpu.VMEM((deep, depth), f32),
            pltpu.VMEM((depth // 128, half, 128), f32),
            pltpu.VMEM((sections, coarse, depth), f32),
            pltpu.VMEM((sections, coarse + 8, depth), f32),
            pltpu.VMEM((sections, 8, depth), f32),
            dma((stages, 2)), dma((stages, 2)), dma((stages, 2, 2)), dma((stages, 2, 2)),
            dma((4 * planes,)), dma((4 * planes,)), dma((9 + planes,)), dma((planes,)), dma((planes,)),
            dma((sections,)), dma((sections,)), dma((sections,)), dma((sections,)),
            dma((sections,)), dma((sections,)),
            pltpu.VMEM((2, planes, half, depth), f32),
            pltpu.VMEM((2, 2, planes, half, depth), f32),
            pltpu.VMEM((planes, half, depth), f32),
            pltpu.VMEM((2, planes, half, depth), f32),
        ],
        compiler_params=pltpu.CompilerParams(
            collective_id=0, has_side_effects=True, vmem_limit_bytes=63 * 1024 * 1024
        ),
        cost_estimate=pl.CostEstimate(
            flops=400 * planes * rows * depth, bytes_accessed=3_000_000, transcendentals=0),
    )(chi_final, psi_late, psi_early, trap, controls)
    chi_start, grad_rows = pl.pallas_call(
        finish_kernel,
        out_shape=(
            jax.ShapeDtypeStruct(chi_final.shape, f32),
            jax.ShapeDtypeStruct(controls.shape, f32),
        ),
        in_specs=[anywhere] * 2,
        out_specs=(anywhere, anywhere),
        scratch_shapes=[
            pltpu.VMEM(chi_final.shape, f32),
            pltpu.VMEM(controls.shape, f32),
            dma((2, 2 * planes + 1)),
        ],
        compiler_params=pltpu.CompilerParams(vmem_limit_bytes=63 * 1024 * 1024),
    )(chi_start, grad_rows)
    return chi_start, grad_rows, power


def solution(mesh):
    placed = (
        P(None, ("starts", "gx"), "gy", None),
        P(None, ("starts", "gx"), "gy", None),
        P(None, ("starts", "gx"), "gy", None),
        P("gx", "gy", None),
        P("starts", "gy", None),
    )
    return jax.shard_map(
        on_device,
        mesh=mesh,
        in_specs=placed,
        out_specs=(P(None, ("starts", "gx"), "gy", None), P("starts", "gy", None), P("starts")),
        check_vma=False,
    )
```

```python
import functools
import math

import jax
import jax.numpy as jnp
from jax import lax
from jax.experimental import pallas as pl
from jax.experimental.pallas import tpu as pltpu
from jax.sharding import PartitionSpec as P

STEP_SIZE = 0.2
MESH = pl.DeviceIdType.MESH


def kernel(
    sections, planes, rows, chi, psi_late, psi_early, trap, controls,
    out, grad, power,
    field, psi, pot, coef, edge_in, edge_out, rim_in, rim_out, result, fine, ctl, prof, folded,
    late_rows, early_rows, far_power,
    x_send, x_recv, y_send, y_recv, t_send, t_recv, own_sem, o_send, o_recv,
    l_send, l_recv, e_send, e_recv, f_send, f_recv, give_chi, give_psi, give_trap, back,
):
    deep, half, coarse = 2 * planes, rows // 2, rows // 4
    depth = chi.shape[3]
    pieces = depth // 128
    group = 2 * sections
    start = lax.axis_index("starts")
    g = lax.axis_index("gx")
    c = lax.axis_index("gy")
    x = lax.rem(g, 2)
    upper = lax.rem(x + c, 2)
    partner = g + 1 - 2 * x
    mine_at = pl.multiple_of(upper * half, half)
    other_at = pl.multiple_of((1 - upper) * half, half)
    mine_planes = x * planes
    other_planes = (1 - x) * planes
    has_low = g >= 2
    has_high = g < sections - 2

    def remote(src, dst, send, recv, to_g, to_c):
        return pltpu.make_async_remote_copy(
            src_ref=src, dst_ref=dst, send_sem=send, recv_sem=recv,
            device_id=(start, to_g, to_c), device_id_type=MESH,
        )

    mine = pl.ds(mine_at, half)
    own = [
        pltpu.make_async_copy(
            chi.at[:, :, mine, :], field.at[0, :, pl.ds(1 + mine_planes, planes)], own_sem.at[0]),
        pltpu.make_async_copy(
            psi_late.at[:, :, mine, :], psi.at[0, :, pl.ds(mine_planes, planes)], own_sem.at[1]),
        pltpu.make_async_copy(
            trap.at[:, mine, :], pot.at[pl.ds(mine_planes, planes)], own_sem.at[2]),
        pltpu.make_async_copy(
            psi_early.at[:, :, mine, :], psi.at[1, :, pl.ds(mine_planes, planes)], own_sem.at[3]),
        pltpu.make_async_copy(controls, ctl, own_sem.at[4]),
    ]
    theirs = pl.ds(other_at, half)
    staged = [
        pltpu.make_async_copy(chi.at[:, :, theirs, :], give_chi, own_sem.at[5]),
        pltpu.make_async_copy(psi_late.at[:, :, theirs, :], give_psi.at[0], own_sem.at[6]),
        pltpu.make_async_copy(trap.at[:, theirs, :], give_trap, own_sem.at[7]),
        pltpu.make_async_copy(psi_early.at[:, :, theirs, :], give_psi.at[1], own_sem.at[8]),
    ]
    for copy in staged:
        copy.start()
    for copy in own:
        copy.start()

    barrier = pltpu.get_barrier_semaphore()
    here = 2 * g + c

    def greet(d, _):
        there = lax.rem(here + d, group)
        pl.semaphore_signal(
            barrier, inc=1, device_id=(start, there // 2, lax.rem(there, 2)), device_id_type=MESH)
        return 0

    lax.fori_loop(1, group, greet, 0)
    pl.semaphore_wait(barrier, group - 1)

    for copy in staged:
        copy.wait()

    def trade(src, dst, i):
        return remote(src, dst, t_send.at[i], t_recv.at[i], partner, c)

    def trades(at, flag):
        moves = []
        for i in range(planes):
            j = i + flag * (planes - 1 - 2 * i)
            moves.append([
                trade(give_chi.at[:, j], field.at[0, :, 1 + at + j], 4 * i),
                trade(give_psi.at[0, :, j], psi.at[0, :, at + j], 4 * i + 1),
                trade(give_trap.at[j], pot.at[at + j], 4 * i + 2),
                trade(give_psi.at[1, :, j], psi.at[1, :, at + j], 4 * i + 3),
            ])
        return moves

    sent = trades(mine_planes, x)
    arriving = trades(other_planes, 1 - x)
    queue = [sent[0][0], sent[1][0], sent[0][1], sent[0][2]]
    queue += [sent[i][0] for i in range(2, planes)]
    for i in range(1, planes):
        queue += [sent[i][1], sent[i][2]]
    queue += [sent[i][3] for i in range(planes)]
    bulk = len(queue) - planes
    flying = 3
    for copy in queue[:flying]:
        copy.start()

    def advance(first, last):
        for i in range(first, last):
            queue[i - flying].wait_send()
            queue[i].start()

    stages = field.shape[0]
    blank = jnp.zeros((half, depth), jnp.float32)

    @pl.when(jnp.logical_not(has_low))
    def _():
        for s in range(stages):
            field[s, 0, 0] = blank
            field[s, 1, 0] = blank

    @pl.when(jnp.logical_not(has_high))
    def _():
        for s in range(stages):
            field[s, 0, deep + 1] = blank
            field[s, 1, deep + 1] = blank

    @pl.when(x == 0)
    def _():
        for s in range(stages):
            edge_in[s, upper] = jnp.zeros((2, deep, depth), jnp.float32)
            rim_in[s, upper] = jnp.zeros((8, depth), jnp.float32)

    def low_copy(s):
        return remote(field.at[s, :, 1], field.at[s, :, deep + 1],
                      x_send.at[s, 0], x_recv.at[s, 1], g - 2, c)

    def high_copy(s):
        return remote(field.at[s, :, deep], field.at[s, :, 0],
                      x_send.at[s, 1], x_recv.at[s, 0], g + 2, c)

    boxes = ((edge_out, edge_in), (rim_out, rim_in))

    def pair_copy(s, box):
        source, target = boxes[box]
        return remote(source.at[s, 1 - upper], target.at[s, upper],
                      y_send.at[s, box, 0], y_recv.at[s, box, 0], partner, c)

    def core_copy(s, box):
        source, target = boxes[box]
        return remote(source.at[s, upper], target.at[s, 1 - upper],
                      y_send.at[s, box, 1], y_recv.at[s, box, 1], g, 1 - c)

    def pair_arrival(s, box):
        source, target = boxes[box]
        return remote(source.at[s, 1 - upper], target.at[s, 1 - upper],
                      y_send.at[s, box, 0], y_recv.at[s, box, 0], partner, c)

    def core_arrival(s, box):
        source, target = boxes[box]
        return remote(source.at[s, upper], target.at[s, upper],
                      y_send.at[s, box, 1], y_recv.at[s, box, 1], g, 1 - c)

    def send_low(s):
        @pl.when(has_low)
        def _():
            low_copy(s).start()

    def send_high(s):
        @pl.when(has_high)
        def _():
            high_copy(s).start()

    def send_edges(s, box):
        pair_copy(s, box).start()

        @pl.when(x == 1)
        def _():
            core_copy(s, box).start()

    def wait_edges(s, box):
        pair_arrival(s, box).wait_recv()

        @pl.when(x == 1)
        def _():
            core_arrival(s, box).wait_recv()

    def wait_low(s):
        @pl.when(has_low)
        def _():
            high_copy(s).wait_recv()

    def wait_high(s):
        @pl.when(has_high)
        def _():
            low_copy(s).wait_recv()

    def settle(s):
        for box in range(2):
            pair_copy(s, box).wait_send()

        @pl.when(x == 1)
        def _():
            for box in range(2):
                core_copy(s, box).wait_send()

        @pl.when(has_low)
        def _():
            low_copy(s).wait_send()

        @pl.when(has_high)
        def _():
            high_copy(s).wait_send()

    index = (g // 2) * deep + lax.broadcasted_iota(jnp.int32, (deep, depth), 0)
    prof[...] = 1.0 + 0.5 * jnp.cos(
        (2.0 * math.pi / (sections * planes)) * index.astype(jnp.float32))
    own[4].wait()
    for k in range(2):
        part = ctl[1 - k, pl.ds(pl.multiple_of(upper * coarse, coarse), coarse), :]
        for m in range(pieces):
            piece = part[:, m * 128:(m + 1) * 128]
            fine[k, m, pl.ds(0, coarse, stride=2), :] = piece
            fine[k, m, pl.ds(1, coarse, stride=2), :] = piece

    def coefficients(k, first, count):
        control = jnp.concatenate([fine[k, m] for m in range(pieces)], axis=1)

        def body(i, _):
            j = first + i
            p = psi[k, 0, j]
            q = psi[k, 1, j]
            base = pot[j] + prof[pl.ds(j, 1), :] * control + 3.0
            p2 = p * p
            q2 = q * q
            both = base + p2 + q2
            coef[k, 0, j] = 2.0 * both + 4.0 * p2
            coef[k, 1, j] = 4.0 * (p * q)
            coef[k, 2, j] = 2.0 * both + 4.0 * q2
            return 0

        lax.fori_loop(0, count, body, 0)

    row = lax.broadcasted_iota(jnp.int32, (8, depth), 0)
    first_row, last_row = row == 0, row == 7
    lane = lax.broadcasted_iota(jnp.int32, (half, 128), 1)
    first_lane, last_lane = lane == 0, lane == 127

    def edge_row(s, side, part, at, end):
        if end is None:
            return edge_in[s, side, part, pl.ds(at - 1, 1), :]
        return rim_in[s, side, pl.ds(2 * part + end, 1), :]

    def neighbours(s, part, at, v, end):
        total = field[s, part, at - 1] + field[s, part, at + 1]
        blocks = [v[i * 8:(i + 1) * 8] for i in range(half // 8)]
        down = [edge_row(s, 0, part, at, end)] + [pltpu.roll(t, 1, 0) for t in blocks]
        up = [pltpu.roll(t, 7, 0) for t in blocks] + [edge_row(s, 1, part, at, end)]
        beside = [
            jnp.where(first_row, down[i], down[i + 1]) + jnp.where(last_row, up[i + 1], up[i])
            for i in range(half // 8)
        ]
        total = total + jnp.concatenate(beside, axis=0)
        blocks = [v[:, i * 128:(i + 1) * 128] for i in range(pieces)]
        down = [0.0] + [pltpu.roll(t, 1, 1) for t in blocks]
        up = [pltpu.roll(t, 127, 1) for t in blocks] + [0.0]
        beside = [
            jnp.where(first_lane, down[i], down[i + 1]) + jnp.where(last_lane, up[i + 1], up[i])
            for i in range(pieces)
        ]
        return total + jnp.concatenate(beside, axis=1)

    def term(s, at, end):
        k, n = s // 4, s % 4
        a = field[s, 0, at]
        b = field[s, 1, at]
        diag_a, mixed, diag_b = coef[k, 0, at - 1], coef[k, 1, at - 1], coef[k, 2, at - 1]
        up = diag_a * a + mixed * b - neighbours(s, 0, at, a, end)
        low = mixed * a + diag_b * b - neighbours(s, 1, at, b, end)
        scale = 0.5 * STEP_SIZE / (n + 1)
        a, b = low * -scale, up * scale
        if n == 3:
            for m in (3, 2, 1, 0):
                a += field[4 * k + m, 0, at]
                b += field[4 * k + m, 1, at]
        return a, b

    def put_edges(s, at, a, b, end):
        for part, v in ((0, a), (1, b)):
            if end is None:
                edge_out[s, 0, part, pl.ds(at - 1, 1), :] = v[0:1]
                edge_out[s, 1, part, pl.ds(at - 1, 1), :] = v[half - 1:half]
            else:
                rim_out[s, 0, pl.ds(2 * part + end, 1), :] = v[0:1]
                rim_out[s, 1, pl.ds(2 * part + end, 1), :] = v[half - 1:half]

    def overlap(k, at, a, b):
        weight = prof[pl.ds(at - 1, 1), :]
        return weight * (a * psi[k, 1, at - 1] - b * psi[k, 0, at - 1])

    def update(s, at, acc, end=None):
        a, b = term(s, at, end)
        field[s + 1, 0, at] = a
        field[s + 1, 1, at] = b
        put_edges(s + 1, at, a, b, end)
        if s == 3:
            acc = acc + overlap(0, at, a, b)
        return acc

    def fold(acc):
        for m in range(pieces):
            folded[m] = acc[:, m * 128:(m + 1) * 128]
        return jnp.concatenate(
            [folded[m, pl.ds(0, coarse, stride=2), :] + folded[m, pl.ds(1, coarse, stride=2), :]
             for m in range(pieces)], axis=1)

    own[0].wait()
    own[1].wait()
    own[2].wait()
    coefficients(0, mine_planes, planes)
    advance(flying, 5)
    arriving[0][0].wait_recv()
    send_low(0)
    send_high(0)
    put_edges(0, 1, field[0, 0, 1], field[0, 1, 1], 0)
    put_edges(0, deep, field[0, 0, deep], field[0, 1, deep], 1)
    send_edges(0, 1)
    advance(5, 7)
    arriving[1][0].wait_recv()
    arriving[0][1].wait_recv()
    arriving[0][2].wait_recv()
    coefficients(0, (1 - x) * (deep - 1), 1)

    def first_edges(at, _):
        put_edges(0, at, field[0, 0, at], field[0, 1, at], None)
        return 0

    late_sends = lambda d: remote(
        late_rows.at[g], late_rows.at[g], l_send.at[d], l_recv.at[g], lax.rem(g + d, sections), c)
    late_arrival = lambda d: remote(
        late_rows.at[g], late_rows.at[lax.rem(g + d, sections)], l_send.at[d],
        l_recv.at[lax.rem(g + d, sections)], lax.rem(g + d, sections), c)

    def loop(count, action):
        def body(d, _):
            action(d)
            return 0

        lax.fori_loop(1, count, body, 0)

    def total(source, parity):
        value = source[parity, 0:coarse]
        return lax.fori_loop(
            1, sections // 2, lambda i, t: t + source[2 * i + parity, 0:coarse], value)

    for s in range(stages - 1):
        if s == 0:
            advance(7, 8)
        acc = blank if s == 3 else 0
        wait_edges(s, 1)
        wait_low(s)
        acc = update(s, 1, acc, 0)
        send_low(s + 1)
        wait_high(s)
        acc = update(s, deep, acc, 1)
        send_high(s + 1)
        send_edges(s + 1, 1)
        if 1 <= s < planes:
            advance(bulk + s, bulk + s + 1)
        if s == 0:
            for i in range(2, planes):
                arriving[i][0].wait_recv()
            lax.fori_loop(2, deep, first_edges, 0)
            send_edges(0, 0)
            for i in range(1, planes):
                advance(min(planes + 2 + 2 * i, bulk), min(planes + 4 + 2 * i, bulk))
                arriving[i][1].wait_recv()
                arriving[i][2].wait_recv()
                coefficients(0, (1 - x) * (deep - 1) + i * (2 * x - 1), 1)
            advance(bulk, bulk + 1)
        wait_edges(s, 0)

        def two(i, acc, s=s):
            acc = update(s, 2 + 2 * i, acc)
            return update(s, 3 + 2 * i, acc)

        acc = lax.fori_loop(0, planes - 1, two, acc)
        send_edges(s + 1, 0)
        settle(s)
        if s == 4:
            for copy in queue[-flying:]:
                copy.wait_send()
        if s == 6:
            loop(sections, lambda d: late_arrival(d).wait_recv())
            loop(sections, lambda d: late_sends(d).wait_send())
            for i, parity in enumerate((c, 1 - c)):
                grad[1, i * coarse:(i + 1) * coarse] = total(late_rows, parity)
        if s == 3:
            late_rows[g] = fold(acc)
            loop(sections, lambda d: late_sends(d).start())
            own[3].wait()
            coefficients(1, mine_planes, planes)
            for j in range(planes):
                arriving[j][3].wait_recv()
            coefficients(1, other_planes, planes)

    s = stages - 1

    def give(j):
        return remote(result.at[:, other_planes + j], back.at[:, j],
                      o_send.at[j], o_recv.at[j], partner, c)

    def put_back(j):
        return pltpu.make_async_copy(back.at[:, j], out.at[:, j, theirs, :], own_sem.at[9 + j])

    def finish(at, accs, end=None):
        acc, square = accs
        a, b = term(s, at, end)
        result[0, at - 1] = a
        result[1, at - 1] = b
        return acc + overlap(1, at, a, b), square + (a * a + b * b)

    accs = (blank, blank)
    wait_edges(s, 0)
    inner_other = other_planes + x
    inner_mine = mine_planes + 1 - x

    def finish_send(i, accs):
        accs = finish(inner_other + i + 1, accs)
        give(x + i).start()
        return accs

    accs = lax.fori_loop(0, planes - 1, finish_send, accs)
    accs = lax.fori_loop(0, planes - 1, lambda i, t: finish(inner_mine + i + 1, t), accs)
    wait_edges(s, 1)
    wait_low(s)
    wait_high(s)
    accs = finish((1 - x) * (deep - 1) + 1, accs, 1 - x)
    give((1 - x) * (planes - 1)).start()
    accs = finish(x * (deep - 1) + 1, accs, x)
    keep = pltpu.make_async_copy(
        result.at[:, pl.ds(mine_planes, planes)], out.at[:, :, mine, :], own_sem.at[0])
    keep.start()
    acc, square = accs
    early_rows[g, 0:coarse] = fold(acc)
    early_rows[g, coarse:coarse + 8] = jnp.sum(square.reshape(half // 8, 8, depth), axis=0)

    def early_copy(d, slot):
        return remote(early_rows.at[g], early_rows.at[slot], e_send.at[d], e_recv.at[slot],
                      lax.rem(g + d, sections), c)

    def far_copy(d, slot):
        return remote(early_rows.at[g, pl.ds(coarse, 8)], far_power.at[slot], f_send.at[d],
                      f_recv.at[slot], lax.rem(g + d, sections), 1 - c)

    far_copy(0, g).start()
    loop(sections, lambda d: (early_copy(d, g).start(), far_copy(d, g).start()))

    settle(s)
    for j in range(planes):
        give(j).wait_send()
    for j in range(planes):
        give(j).wait_recv()
        put_back(j).start()
    far_copy(0, g).wait_recv()
    loop(sections, lambda d: (
        early_copy(d, lax.rem(g + d, sections)).wait_recv(),
        far_copy(d, lax.rem(g + d, sections)).wait_recv()))

    def squares(i, t):
        near, far = t
        return near + early_rows[i, coarse:coarse + 8], far + far_power[i]

    zero = jnp.zeros((8, depth), jnp.float32)
    near, far = lax.fori_loop(0, sections, squares, (zero, zero))
    mean = jnp.sum(near + far) / float(sections * planes * 2 * rows * depth)
    power[0] = mean
    scale = jnp.sqrt(float(sections * planes) * (jnp.full((coarse, depth), mean) + 1e-06))
    early = [total(early_rows, c), total(early_rows, 1 - c)]
    for i in range(2):
        grad[0, i * coarse:(i + 1) * coarse] = early[i] / scale
        grad[1, i * coarse:(i + 1) * coarse] = grad[1, i * coarse:(i + 1) * coarse] / scale

    loop(sections, lambda d: (early_copy(d, g).wait_send(), far_copy(d, g).wait_send()))
    far_copy(0, g).wait_send()
    keep.wait()
    for j in range(planes):
        put_back(j).wait()


def finish_kernel(field_in, grad_in, field_out, grad_out, held, held_grad, sems):
    planes = field_in.shape[1]
    moves = [(grad_in, held_grad, grad_out)]
    for part in range(2):
        for j in range(planes):
            moves.append((field_in.at[part, j], held.at[part, j], field_out.at[part, j]))
    arrive = [pltpu.make_async_copy(a, b, sems.at[0, i]) for i, (a, b, _) in enumerate(moves)]
    leave = [pltpu.make_async_copy(b, o, sems.at[1, i]) for i, (_, b, o) in enumerate(moves)]
    for copy in arrive:
        copy.start()
    for copy, then in zip(arrive, leave):
        copy.wait()
        then.start()
    for copy in leave:
        copy.wait()


def on_device(chi_final, psi_late, psi_early, trap, controls):
    planes, rows, depth = chi_final.shape[1:]
    sections = lax.axis_size("gx")
    deep, half, coarse = 2 * planes, rows // 2, rows // 4
    stages = 8
    f32 = jnp.float32
    anywhere = pl.BlockSpec(memory_space=pltpu.HBM)
    dma = pltpu.SemaphoreType.DMA
    chi_start, grad_rows, power = pl.pallas_call(
        functools.partial(kernel, sections, planes, rows),
        out_shape=(
            jax.ShapeDtypeStruct(chi_final.shape, f32),
            jax.ShapeDtypeStruct(controls.shape, f32),
            jax.ShapeDtypeStruct((1,), f32),
        ),
        in_specs=[anywhere] * 5,
        out_specs=(
            anywhere,
            pl.BlockSpec(memory_space=pltpu.VMEM),
            pl.BlockSpec(memory_space=pltpu.SMEM),
        ),
        scratch_shapes=[
            pltpu.VMEM((stages, 2, deep + 2, half, depth), f32),
            pltpu.VMEM((2, 2, deep, half, depth), f32),
            pltpu.VMEM((deep, half, depth), f32),
            pltpu.VMEM((2, 3, deep, half, depth), f32),
            pltpu.VMEM((stages, 2, 2, deep, depth), f32),
            pltpu.VMEM((stages, 2, 2, deep, depth), f32),
            pltpu.VMEM((stages, 2, 8, depth), f32),
            pltpu.VMEM((stages, 2, 8, depth), f32),
            pltpu.VMEM((2, deep, half, depth), f32),
            pltpu.VMEM((2, depth // 128, half, 128), f32),
            pltpu.VMEM(controls.shape, f32),
            pltpu.VMEM((deep, depth), f32),
            pltpu.VMEM((depth // 128, half, 128), f32),
            pltpu.VMEM((sections, coarse, depth), f32),
            pltpu.VMEM((sections, coarse + 8, depth), f32),
            pltpu.VMEM((sections, 8, depth), f32),
            dma((stages, 2)), dma((stages, 2)), dma((stages, 2, 2)), dma((stages, 2, 2)),
            dma((4 * planes,)), dma((4 * planes,)), dma((9 + planes,)), dma((planes,)), dma((planes,)),
            dma((sections,)), dma((sections,)), dma((sections,)), dma((sections,)),
            dma((sections,)), dma((sections,)),
            pltpu.VMEM((2, planes, half, depth), f32),
            pltpu.VMEM((2, 2, planes, half, depth), f32),
            pltpu.VMEM((planes, half, depth), f32),
            pltpu.VMEM((2, planes, half, depth), f32),
        ],
        compiler_params=pltpu.CompilerParams(
            collective_id=0, has_side_effects=True, vmem_limit_bytes=63 * 1024 * 1024
        ),
        cost_estimate=pl.CostEstimate(
            flops=400 * planes * rows * depth, bytes_accessed=3_000_000, transcendentals=0),
    )(chi_final, psi_late, psi_early, trap, controls)
    chi_start, grad_rows = pl.pallas_call(
        finish_kernel,
        out_shape=(
            jax.ShapeDtypeStruct(chi_final.shape, f32),
            jax.ShapeDtypeStruct(controls.shape, f32),
        ),
        in_specs=[anywhere] * 2,
        out_specs=(anywhere, anywhere),
        scratch_shapes=[
            pltpu.VMEM(chi_final.shape, f32),
            pltpu.VMEM(controls.shape, f32),
            dma((2, 2 * planes + 1)),
        ],
        compiler_params=pltpu.CompilerParams(vmem_limit_bytes=63 * 1024 * 1024),
    )(chi_start, grad_rows)
    return chi_start, grad_rows, power


def solution(mesh):
    placed = (
        P(None, ("starts", "gx"), "gy", None),
        P(None, ("starts", "gx"), "gy", None),
        P(None, ("starts", "gx"), "gy", None),
        P("gx", "gy", None),
        P("starts", "gy", None),
    )
    return jax.shard_map(
        on_device,
        mesh=mesh,
        in_specs=placed,
        out_specs=(P(None, ("starts", "gx"), "gy", None), P("starts", "gy", None), P("starts")),
        check_vma=False,
    )
```

```python
import functools
import math

import jax
import jax.numpy as jnp
from jax import lax
from jax.experimental import pallas as pl
from jax.experimental.pallas import tpu as pltpu
from jax.sharding import PartitionSpec as P

STEP_SIZE = 0.2
MESH = pl.DeviceIdType.MESH


def kernel(
    sections, planes, rows, chi, psi_late, psi_early, trap, controls,
    out, grad, power,
    field, psi, pot, coef, edge_in, edge_out, rim_in, rim_out, result, fine, ctl, prof, folded,
    late_rows, early_rows, far_power,
    x_send, x_recv, y_send, y_recv, t_send, t_recv, own_sem, o_send, o_recv,
    l_send, l_recv, e_send, e_recv, f_send, f_recv, give_chi, give_psi, give_trap, back,
):
    deep, half, coarse = 2 * planes, rows // 2, rows // 4
    depth = chi.shape[3]
    pieces = depth // 128
    group = 2 * sections
    start = lax.axis_index("starts")
    g = lax.axis_index("gx")
    c = lax.axis_index("gy")
    x = lax.rem(g, 2)
    upper = lax.rem(x + c, 2)
    partner = g + 1 - 2 * x
    mine_at = pl.multiple_of(upper * half, half)
    other_at = pl.multiple_of((1 - upper) * half, half)
    mine_planes = x * planes
    other_planes = (1 - x) * planes
    has_low = g >= 2
    has_high = g < sections - 2

    def remote(src, dst, send, recv, to_g, to_c):
        return pltpu.make_async_remote_copy(
            src_ref=src, dst_ref=dst, send_sem=send, recv_sem=recv,
            device_id=(start, to_g, to_c), device_id_type=MESH,
        )

    mine = pl.ds(mine_at, half)
    own = [
        pltpu.make_async_copy(
            chi.at[:, :, mine, :], field.at[0, :, pl.ds(1 + mine_planes, planes)], own_sem.at[0]),
        pltpu.make_async_copy(
            psi_late.at[:, :, mine, :], psi.at[0, :, pl.ds(mine_planes, planes)], own_sem.at[1]),
        pltpu.make_async_copy(
            trap.at[:, mine, :], pot.at[pl.ds(mine_planes, planes)], own_sem.at[2]),
        pltpu.make_async_copy(
            psi_early.at[:, :, mine, :], psi.at[1, :, pl.ds(mine_planes, planes)], own_sem.at[3]),
        pltpu.make_async_copy(controls, ctl, own_sem.at[4]),
    ]
    theirs = pl.ds(other_at, half)
    staged = [
        pltpu.make_async_copy(chi.at[:, :, theirs, :], give_chi, own_sem.at[5]),
        pltpu.make_async_copy(psi_late.at[:, :, theirs, :], give_psi.at[0], own_sem.at[6]),
        pltpu.make_async_copy(trap.at[:, theirs, :], give_trap, own_sem.at[7]),
        pltpu.make_async_copy(psi_early.at[:, :, theirs, :], give_psi.at[1], own_sem.at[8]),
    ]
    for copy in staged:
        copy.start()
    for copy in own:
        copy.start()

    barrier = pltpu.get_barrier_semaphore()
    here = 2 * g + c

    def greet(d, _):
        there = lax.rem(here + d, group)
        pl.semaphore_signal(
            barrier, inc=1, device_id=(start, there // 2, lax.rem(there, 2)), device_id_type=MESH)
        return 0

    lax.fori_loop(1, group, greet, 0)
    pl.semaphore_wait(barrier, group - 1)

    for copy in staged:
        copy.wait()

    def trade(src, dst, i):
        return remote(src, dst, t_send.at[i], t_recv.at[i], partner, c)

    def trades(at, flag):
        moves = []
        for i in range(planes):
            j = i + flag * (planes - 1 - 2 * i)
            moves.append([
                trade(give_chi.at[:, j], field.at[0, :, 1 + at + j], 4 * i),
                trade(give_psi.at[0, :, j], psi.at[0, :, at + j], 4 * i + 1),
                trade(give_trap.at[j], pot.at[at + j], 4 * i + 2),
                trade(give_psi.at[1, :, j], psi.at[1, :, at + j], 4 * i + 3),
            ])
        return moves

    sent = trades(mine_planes, x)
    arriving = trades(other_planes, 1 - x)
    queue = [sent[0][0], sent[1][0], sent[0][1], sent[0][2]]
    queue += [sent[i][0] for i in range(2, planes)]
    for i in range(1, planes):
        queue += [sent[i][1], sent[i][2]]
    queue += [sent[i][3] for i in range(planes)]
    bulk = len(queue) - planes
    flying = 2
    for copy in queue[:flying]:
        copy.start()

    def advance(first, last):
        for i in range(first, last):
            queue[i - flying].wait_send()
            queue[i].start()

    stages = field.shape[0]
    blank = jnp.zeros((half, depth), jnp.float32)

    @pl.when(jnp.logical_not(has_low))
    def _():
        for s in range(stages):
            field[s, 0, 0] = blank
            field[s, 1, 0] = blank

    @pl.when(jnp.logical_not(has_high))
    def _():
        for s in range(stages):
            field[s, 0, deep + 1] = blank
            field[s, 1, deep + 1] = blank

    @pl.when(x == 0)
    def _():
        for s in range(stages):
            edge_in[s, upper] = jnp.zeros((2, deep, depth), jnp.float32)
            rim_in[s, upper] = jnp.zeros((8, depth), jnp.float32)

    def low_copy(s):
        return remote(field.at[s, :, 1], field.at[s, :, deep + 1],
                      x_send.at[s, 0], x_recv.at[s, 1], g - 2, c)

    def high_copy(s):
        return remote(field.at[s, :, deep], field.at[s, :, 0],
                      x_send.at[s, 1], x_recv.at[s, 0], g + 2, c)

    boxes = ((edge_out, edge_in), (rim_out, rim_in))

    def pair_copy(s, box):
        source, target = boxes[box]
        return remote(source.at[s, 1 - upper], target.at[s, upper],
                      y_send.at[s, box, 0], y_recv.at[s, box, 0], partner, c)

    def core_copy(s, box):
        source, target = boxes[box]
        return remote(source.at[s, upper], target.at[s, 1 - upper],
                      y_send.at[s, box, 1], y_recv.at[s, box, 1], g, 1 - c)

    def pair_arrival(s, box):
        source, target = boxes[box]
        return remote(source.at[s, 1 - upper], target.at[s, 1 - upper],
                      y_send.at[s, box, 0], y_recv.at[s, box, 0], partner, c)

    def core_arrival(s, box):
        source, target = boxes[box]
        return remote(source.at[s, upper], target.at[s, upper],
                      y_send.at[s, box, 1], y_recv.at[s, box, 1], g, 1 - c)

    def send_low(s):
        @pl.when(has_low)
        def _():
            low_copy(s).start()

    def send_high(s):
        @pl.when(has_high)
        def _():
            high_copy(s).start()

    def send_edges(s, box):
        pair_copy(s, box).start()

        @pl.when(x == 1)
        def _():
            core_copy(s, box).start()

    def wait_edges(s, box):
        pair_arrival(s, box).wait_recv()

        @pl.when(x == 1)
        def _():
            core_arrival(s, box).wait_recv()

    def wait_low(s):
        @pl.when(has_low)
        def _():
            high_copy(s).wait_recv()

    def wait_high(s):
        @pl.when(has_high)
        def _():
            low_copy(s).wait_recv()

    def settle(s):
        for box in range(2):
            pair_copy(s, box).wait_send()

        @pl.when(x == 1)
        def _():
            for box in range(2):
                core_copy(s, box).wait_send()

        @pl.when(has_low)
        def _():
            low_copy(s).wait_send()

        @pl.when(has_high)
        def _():
            high_copy(s).wait_send()

    index = (g // 2) * deep + lax.broadcasted_iota(jnp.int32, (deep, depth), 0)
    prof[...] = 1.0 + 0.5 * jnp.cos(
        (2.0 * math.pi / (sections * planes)) * index.astype(jnp.float32))
    own[4].wait()
    for k in range(2):
        part = ctl[1 - k, pl.ds(pl.multiple_of(upper * coarse, coarse), coarse), :]
        for m in range(pieces):
            piece = part[:, m * 128:(m + 1) * 128]
            fine[k, m, pl.ds(0, coarse, stride=2), :] = piece
            fine[k, m, pl.ds(1, coarse, stride=2), :] = piece

    def coefficients(k, first, count):
        control = jnp.concatenate([fine[k, m] for m in range(pieces)], axis=1)

        def body(i, _):
            j = first + i
            p = psi[k, 0, j]
            q = psi[k, 1, j]
            base = pot[j] + prof[pl.ds(j, 1), :] * control + 3.0
            p2 = p * p
            q2 = q * q
            both = base + p2 + q2
            coef[k, 0, j] = 2.0 * both + 4.0 * p2
            coef[k, 1, j] = 4.0 * (p * q)
            coef[k, 2, j] = 2.0 * both + 4.0 * q2
            return 0

        lax.fori_loop(0, count, body, 0)

    row = lax.broadcasted_iota(jnp.int32, (8, depth), 0)
    first_row, last_row = row == 0, row == 7
    lane = lax.broadcasted_iota(jnp.int32, (half, 128), 1)
    first_lane, last_lane = lane == 0, lane == 127

    def edge_row(s, side, part, at, end):
        if end is None:
            return edge_in[s, side, part, pl.ds(at - 1, 1), :]
        return rim_in[s, side, pl.ds(2 * part + end, 1), :]

    def neighbours(s, part, at, v, end):
        total = field[s, part, at - 1] + field[s, part, at + 1]
        blocks = [v[i * 8:(i + 1) * 8] for i in range(half // 8)]
        down = [edge_row(s, 0, part, at, end)] + [pltpu.roll(t, 1, 0) for t in blocks]
        up = [pltpu.roll(t, 7, 0) for t in blocks] + [edge_row(s, 1, part, at, end)]
        beside = [
            jnp.where(first_row, down[i], down[i + 1]) + jnp.where(last_row, up[i + 1], up[i])
            for i in range(half // 8)
        ]
        total = total + jnp.concatenate(beside, axis=0)
        blocks = [v[:, i * 128:(i + 1) * 128] for i in range(pieces)]
        down = [0.0] + [pltpu.roll(t, 1, 1) for t in blocks]
        up = [pltpu.roll(t, 127, 1) for t in blocks] + [0.0]
        beside = [
            jnp.where(first_lane, down[i], down[i + 1]) + jnp.where(last_lane, up[i + 1], up[i])
            for i in range(pieces)
        ]
        return total + jnp.concatenate(beside, axis=1)

    def term(s, at, end):
        k, n = s // 4, s % 4
        a = field[s, 0, at]
        b = field[s, 1, at]
        diag_a, mixed, diag_b = coef[k, 0, at - 1], coef[k, 1, at - 1], coef[k, 2, at - 1]
        up = diag_a * a + mixed * b - neighbours(s, 0, at, a, end)
        low = mixed * a + diag_b * b - neighbours(s, 1, at, b, end)
        scale = 0.5 * STEP_SIZE / (n + 1)
        a, b = low * -scale, up * scale
        if n == 3:
            for m in (3, 2, 1, 0):
                a += field[4 * k + m, 0, at]
                b += field[4 * k + m, 1, at]
        return a, b

    def put_edges(s, at, a, b, end):
        for part, v in ((0, a), (1, b)):
            if end is None:
                edge_out[s, 0, part, pl.ds(at - 1, 1), :] = v[0:1]
                edge_out[s, 1, part, pl.ds(at - 1, 1), :] = v[half - 1:half]
            else:
                rim_out[s, 0, pl.ds(2 * part + end, 1), :] = v[0:1]
                rim_out[s, 1, pl.ds(2 * part + end, 1), :] = v[half - 1:half]

    def overlap(k, at, a, b):
        weight = prof[pl.ds(at - 1, 1), :]
        return weight * (a * psi[k, 1, at - 1] - b * psi[k, 0, at - 1])

    def update(s, at, acc, end=None):
        a, b = term(s, at, end)
        field[s + 1, 0, at] = a
        field[s + 1, 1, at] = b
        put_edges(s + 1, at, a, b, end)
        if s == 3:
            acc = acc + overlap(0, at, a, b)
        return acc

    def fold(acc):
        for m in range(pieces):
            folded[m] = acc[:, m * 128:(m + 1) * 128]
        return jnp.concatenate(
            [folded[m, pl.ds(0, coarse, stride=2), :] + folded[m, pl.ds(1, coarse, stride=2), :]
             for m in range(pieces)], axis=1)

    own[0].wait()
    own[1].wait()
    own[2].wait()
    coefficients(0, mine_planes, planes)
    advance(flying, 5)
    arriving[0][0].wait_recv()
    send_low(0)
    send_high(0)
    put_edges(0, 1, field[0, 0, 1], field[0, 1, 1], 0)
    put_edges(0, deep, field[0, 0, deep], field[0, 1, deep], 1)
    send_edges(0, 1)
    advance(5, 7)
    arriving[1][0].wait_recv()
    arriving[0][1].wait_recv()
    arriving[0][2].wait_recv()
    coefficients(0, (1 - x) * (deep - 1), 1)

    def first_edges(at, _):
        put_edges(0, at, field[0, 0, at], field[0, 1, at], None)
        return 0

    late_sends = lambda d: remote(
        late_rows.at[g], late_rows.at[g], l_send.at[d], l_recv.at[g], lax.rem(g + d, sections), c)
    late_arrival = lambda d: remote(
        late_rows.at[g], late_rows.at[lax.rem(g + d, sections)], l_send.at[d],
        l_recv.at[lax.rem(g + d, sections)], lax.rem(g + d, sections), c)

    def loop(count, action):
        def body(d, _):
            action(d)
            return 0

        lax.fori_loop(1, count, body, 0)

    def total(source, parity):
        value = source[parity, 0:coarse]
        return lax.fori_loop(
            1, sections // 2, lambda i, t: t + source[2 * i + parity, 0:coarse], value)

    for s in range(stages - 1):
        if s == 0:
            advance(7, 8)
        acc = blank if s == 3 else 0
        wait_edges(s, 1)
        wait_low(s)
        acc = update(s, 1, acc, 0)
        send_low(s + 1)
        wait_high(s)
        acc = update(s, deep, acc, 1)
        send_high(s + 1)
        send_edges(s + 1, 1)
        if 1 <= s < planes:
            advance(bulk + s, bulk + s + 1)
        if s == 0:
            for i in range(2, planes):
                arriving[i][0].wait_recv()
            lax.fori_loop(2, deep, first_edges, 0)
            send_edges(0, 0)
            for i in range(1, planes):
                advance(min(planes + 2 + 2 * i, bulk), min(planes + 4 + 2 * i, bulk))
                arriving[i][1].wait_recv()
                arriving[i][2].wait_recv()
                coefficients(0, (1 - x) * (deep - 1) + i * (2 * x - 1), 1)
            advance(bulk, bulk + 1)
        wait_edges(s, 0)

        def two(i, acc, s=s):
            acc = update(s, 2 + 2 * i, acc)
            return update(s, 3 + 2 * i, acc)

        acc = lax.fori_loop(0, planes - 1, two, acc)
        send_edges(s + 1, 0)
        settle(s)
        if s == 4:
            for copy in queue[-flying:]:
                copy.wait_send()
        if s == 6:
            loop(sections, lambda d: late_arrival(d).wait_recv())
            loop(sections, lambda d: late_sends(d).wait_send())
            for i, parity in enumerate((c, 1 - c)):
                grad[1, i * coarse:(i + 1) * coarse] = total(late_rows, parity)
        if s == 3:
            late_rows[g] = fold(acc)
            loop(sections, lambda d: late_sends(d).start())
            own[3].wait()
            coefficients(1, mine_planes, planes)
            for j in range(planes):
                arriving[j][3].wait_recv()
            coefficients(1, other_planes, planes)

    s = stages - 1

    def give(j):
        return remote(result.at[:, other_planes + j], back.at[:, j],
                      o_send.at[j], o_recv.at[j], partner, c)

    def put_back(j):
        return pltpu.make_async_copy(back.at[:, j], out.at[:, j, theirs, :], own_sem.at[9 + j])

    def finish(at, accs, end=None):
        acc, square = accs
        a, b = term(s, at, end)
        result[0, at - 1] = a
        result[1, at - 1] = b
        return acc + overlap(1, at, a, b), square + (a * a + b * b)

    accs = (blank, blank)
    wait_edges(s, 0)
    inner_other = other_planes + x
    inner_mine = mine_planes + 1 - x

    def finish_send(i, accs):
        accs = finish(inner_other + i + 1, accs)
        give(x + i).start()
        return accs

    accs = lax.fori_loop(0, planes - 1, finish_send, accs)
    accs = lax.fori_loop(0, planes - 1, lambda i, t: finish(inner_mine + i + 1, t), accs)
    wait_edges(s, 1)
    wait_low(s)
    wait_high(s)
    accs = finish((1 - x) * (deep - 1) + 1, accs, 1 - x)
    give((1 - x) * (planes - 1)).start()
    accs = finish(x * (deep - 1) + 1, accs, x)
    keep = pltpu.make_async_copy(
        result.at[:, pl.ds(mine_planes, planes)], out.at[:, :, mine, :], own_sem.at[0])
    keep.start()
    acc, square = accs
    early_rows[g, 0:coarse] = fold(acc)
    early_rows[g, coarse:coarse + 8] = jnp.sum(square.reshape(half // 8, 8, depth), axis=0)

    def early_copy(d, slot):
        return remote(early_rows.at[g], early_rows.at[slot], e_send.at[d], e_recv.at[slot],
                      lax.rem(g + d, sections), c)

    def far_copy(d, slot):
        return remote(early_rows.at[g, pl.ds(coarse, 8)], far_power.at[slot], f_send.at[d],
                      f_recv.at[slot], lax.rem(g + d, sections), 1 - c)

    far_copy(0, g).start()
    loop(sections, lambda d: (early_copy(d, g).start(), far_copy(d, g).start()))

    settle(s)
    for j in range(planes):
        give(j).wait_send()
    for j in range(planes):
        give(j).wait_recv()
        put_back(j).start()
    far_copy(0, g).wait_recv()
    loop(sections, lambda d: (
        early_copy(d, lax.rem(g + d, sections)).wait_recv(),
        far_copy(d, lax.rem(g + d, sections)).wait_recv()))

    def squares(i, t):
        near, far = t
        return near + early_rows[i, coarse:coarse + 8], far + far_power[i]

    zero = jnp.zeros((8, depth), jnp.float32)
    near, far = lax.fori_loop(0, sections, squares, (zero, zero))
    mean = jnp.sum(near + far) / float(sections * planes * 2 * rows * depth)
    power[0] = mean
    scale = jnp.sqrt(float(sections * planes) * (jnp.full((coarse, depth), mean) + 1e-06))
    early = [total(early_rows, c), total(early_rows, 1 - c)]
    for i in range(2):
        grad[0, i * coarse:(i + 1) * coarse] = early[i] / scale
        grad[1, i * coarse:(i + 1) * coarse] = grad[1, i * coarse:(i + 1) * coarse] / scale

    loop(sections, lambda d: (early_copy(d, g).wait_send(), far_copy(d, g).wait_send()))
    far_copy(0, g).wait_send()
    keep.wait()
    for j in range(planes):
        put_back(j).wait()


def finish_kernel(field_in, grad_in, field_out, grad_out, held, held_grad, sems):
    planes = field_in.shape[1]
    moves = [(grad_in, held_grad, grad_out)]
    for part in range(2):
        for j in range(planes):
            moves.append((field_in.at[part, j], held.at[part, j], field_out.at[part, j]))
    arrive = [pltpu.make_async_copy(a, b, sems.at[0, i]) for i, (a, b, _) in enumerate(moves)]
    leave = [pltpu.make_async_copy(b, o, sems.at[1, i]) for i, (_, b, o) in enumerate(moves)]
    for copy in arrive:
        copy.start()
    for copy, then in zip(arrive, leave):
        copy.wait()
        then.start()
    for copy in leave:
        copy.wait()


def on_device(chi_final, psi_late, psi_early, trap, controls):
    planes, rows, depth = chi_final.shape[1:]
    sections = lax.axis_size("gx")
    deep, half, coarse = 2 * planes, rows // 2, rows // 4
    stages = 8
    f32 = jnp.float32
    anywhere = pl.BlockSpec(memory_space=pltpu.HBM)
    dma = pltpu.SemaphoreType.DMA
    chi_start, grad_rows, power = pl.pallas_call(
        functools.partial(kernel, sections, planes, rows),
        out_shape=(
            jax.ShapeDtypeStruct(chi_final.shape, f32),
            jax.ShapeDtypeStruct(controls.shape, f32),
            jax.ShapeDtypeStruct((1,), f32),
        ),
        in_specs=[anywhere] * 5,
        out_specs=(
            anywhere,
            pl.BlockSpec(memory_space=pltpu.VMEM),
            pl.BlockSpec(memory_space=pltpu.SMEM),
        ),
        scratch_shapes=[
            pltpu.VMEM((stages, 2, deep + 2, half, depth), f32),
            pltpu.VMEM((2, 2, deep, half, depth), f32),
            pltpu.VMEM((deep, half, depth), f32),
            pltpu.VMEM((2, 3, deep, half, depth), f32),
            pltpu.VMEM((stages, 2, 2, deep, depth), f32),
            pltpu.VMEM((stages, 2, 2, deep, depth), f32),
            pltpu.VMEM((stages, 2, 8, depth), f32),
            pltpu.VMEM((stages, 2, 8, depth), f32),
            pltpu.VMEM((2, deep, half, depth), f32),
            pltpu.VMEM((2, depth // 128, half, 128), f32),
            pltpu.VMEM(controls.shape, f32),
            pltpu.VMEM((deep, depth), f32),
            pltpu.VMEM((depth // 128, half, 128), f32),
            pltpu.VMEM((sections, coarse, depth), f32),
            pltpu.VMEM((sections, coarse + 8, depth), f32),
            pltpu.VMEM((sections, 8, depth), f32),
            dma((stages, 2)), dma((stages, 2)), dma((stages, 2, 2)), dma((stages, 2, 2)),
            dma((4 * planes,)), dma((4 * planes,)), dma((9 + planes,)), dma((planes,)), dma((planes,)),
            dma((sections,)), dma((sections,)), dma((sections,)), dma((sections,)),
            dma((sections,)), dma((sections,)),
            pltpu.VMEM((2, planes, half, depth), f32),
            pltpu.VMEM((2, 2, planes, half, depth), f32),
            pltpu.VMEM((planes, half, depth), f32),
            pltpu.VMEM((2, planes, half, depth), f32),
        ],
        compiler_params=pltpu.CompilerParams(
            collective_id=0, has_side_effects=True, vmem_limit_bytes=63 * 1024 * 1024
        ),
        cost_estimate=pl.CostEstimate(
            flops=400 * planes * rows * depth, bytes_accessed=3_000_000, transcendentals=0),
    )(chi_final, psi_late, psi_early, trap, controls)
    chi_start, grad_rows = pl.pallas_call(
        finish_kernel,
        out_shape=(
            jax.ShapeDtypeStruct(chi_final.shape, f32),
            jax.ShapeDtypeStruct(controls.shape, f32),
        ),
        in_specs=[anywhere] * 2,
        out_specs=(anywhere, anywhere),
        scratch_shapes=[
            pltpu.VMEM(chi_final.shape, f32),
            pltpu.VMEM(controls.shape, f32),
            dma((2, 2 * planes + 1)),
        ],
        compiler_params=pltpu.CompilerParams(vmem_limit_bytes=63 * 1024 * 1024),
    )(chi_start, grad_rows)
    return chi_start, grad_rows, power


def solution(mesh):
    placed = (
        P(None, ("starts", "gx"), "gy", None),
        P(None, ("starts", "gx"), "gy", None),
        P(None, ("starts", "gx"), "gy", None),
        P("gx", "gy", None),
        P("starts", "gy", None),
    )
    return jax.shard_map(
        on_device,
        mesh=mesh,
        in_specs=placed,
        out_specs=(P(None, ("starts", "gx"), "gy", None), P("starts", "gy", None), P("starts")),
        check_vma=False,
    )
```
